32 devices in a mesh: groups: 1, tensor: 32 (over z, y, x, core).
Axes of the slice: x: 2, y: 2, z: 4, core: 2. Of those that a mesh axis runs over, the one named last changes fastest.
Arguments:
- tokens: bfloat16 [32, 8192], P(('groups', 'tensor')), may hold values from -6 to 6
- norm_gain: float32 [2, 8192], replicated, may hold values from 0.5 to 1.5
- gate_codes: int32 [2, 2048, 24576], P(None, None, 'tensor'), may hold values from 0 to 255
- up_codes: int32 [2, 2048, 24576], P(None, None, 'tensor'), may hold values from 0 to 255
- down_codes: int32 [2, 6144, 8192], P(None, 'tensor'), may hold values from 0 to 255
- gate_zero: int32 [2, 128, 24576], P(None, None, 'tensor'), may hold values from 0 to 3
- up_zero: int32 [2, 128, 24576], P(None, None, 'tensor'), may hold values from 0 to 3
- down_zero: int32 [2, 384, 8192], P(None, 'tensor'), may hold values from 0 to 3
- gate_step: float32 [2, 128, 24576], P(None, None, 'tensor'), may hold values from 0.00386699 to 0.01546796
- up_step: float32 [2, 128, 24576], P(None, None, 'tensor'), may hold values from 0.00386699 to 0.01546796
- down_step: float32 [2, 384, 8192], P(None, 'tensor'), may hold values from 0.00159472 to 0.00637888
- out_grad: bfloat16 [32, 8192], P(('groups', 'tensor')), may hold values from -6 to 6
- doc_lengths: int32 [4, 3], P('groups'), may hold values from 1 to 4, 8 in all within a row
Outputs:
- input_grad: bfloat16 [32, 8192], P(('groups', 'tensor'))
- gate_step_grad: float32 [2, 128, 24576], P('groups', None, 'tensor')
- up_step_grad: float32 [2, 128, 24576], P('groups', None, 'tensor')
- down_step_grad: float32 [2, 384, 8192], P('groups', 'tensor')
The draws below stay inside these ranges and needn't reach their ends.
Inputs may be any that keep to these rules, and one draw needn't show every extreme that they name: `gate_codes`: each word holds four codes of 0 to 3. `up_codes`: each word holds four codes of 0 to 3. `down_codes`: each word holds four codes of 0 to 3. `doc_lengths`: each row sums to 8.
All inputs are finite; a program needn't handle non-finite values.
Results may differ from the reference program's by a relative error of at most 0.015.
Values may be sent and summed in bfloat16 or wider, within the bound.
No kernel may reach another device: no remote copies, remote signals or barrier semaphores. Data moves between devices by JAX's collectives and lax.ppermute only.
A program may use at most 512 MiB of HBM per device.

```python
import math
import jax
import jax.numpy as jnp
import numpy as np
from jax import lax

D = 8192
FF = 24576
GROUP = 64
LAYERS = 2
MICRO = 4
DOCS = 3
TOKENS = 32
MB_TOK = 8


def with_ends(entries, rng, smallest, largest):
    extent = entries.shape
    place = [jax.random.randint(jax.random.fold_in(rng, axis), (), 0, extent[axis]) for axis in range(len(extent))]
    entries = entries.at[tuple(place)].set(smallest)
    longest = extent.index(max(extent))
    place[longest] = (place[longest] + 1) % extent[longest]
    return entries.at[tuple(place)].set(largest)


def block_levels(stream_key, dims, cuts, low, high):
    def one(dim, shards_of):
        heights = jax.random.uniform(jax.random.fold_in(jax.random.fold_in(stream_key, 6), dim), (shards_of,), jnp.float32, low / len(cuts), high / len(cuts))
        return jnp.repeat(jnp.exp(heights), dims[dim] // shards_of).reshape((-1,) + (1,) * (len(dims) - dim - 1))

    level = one(*cuts[0])
    for cut in cuts[1:]:
        level = level * one(*cut)
    return level


def split_up(amount, total, bound, skew):
    weights = [(1 << 20) // math.isqrt(standing ** skew) + 1 for standing in range(2, amount + 1)]
    spare, given = total - bound - (amount - 1), [1] * (amount - 1)
    while spare > 0:
        free = [i for i in range(amount - 1) if given[i] < bound]
        pool, budget = sum([weights[i] for i in free]), spare
        for i in free:
            more = min(bound - given[i], max(1, budget * weights[i] // pool), spare)
            given[i] = given[i] + more
            spare = spare - more
    return np.array([bound] + given)


def ragged(rng, amount, total, limit, slope):
    if amount == 2:
        one = jax.random.randint(rng, (), max(1, total - limit), min(limit, total - 1) + 1)
        return jnp.stack([one, total - one])
    sizes = jnp.asarray(split_up(amount, total, limit, slope), jnp.int32)
    couples = (amount - 1) // 2
    giver, receiver = sizes[1:1 + 2 * couples:2], sizes[2:2 + 2 * couples:2]
    slack = jnp.minimum(giver - 1, limit - receiver)
    shifted = jax.random.randint(jax.random.fold_in(rng, 1), (couples,), 0, 1 << 20) % (slack + 1)
    sizes = sizes.at[1:1 + 2 * couples:2].set(giver - shifted).at[2:2 + 2 * couples:2].set(receiver + shifted)
    return sizes[jax.random.permutation(jax.random.fold_in(rng, 2), amount)]


def normal_values(rng, dims, spread, bound, cuts=(), held_as=jnp.bfloat16):
    drawn = jax.random.normal(rng, dims, jnp.float32) * spread
    if len(cuts) > 0:
        drawn = block_levels(rng, dims, cuts, -0.22, 0.18) * drawn
    return jnp.clip(drawn, min=-bound, max=bound).astype(held_as)


def setup_inputs(seed: int = 0, part: int = 0) -> dict:
    key_of = jax.random.split(jax.random.key(seed), 14)
    part_keys = jax.random.split(jax.random.fold_in(key_of[13], part), 14)
    return {
        "tokens": normal_values(part_keys[0], (TOKENS, D), 1.0, 6.0, ((0, 32),)),
        "norm_gain": jnp.clip(1.0 + 0.1 * jax.random.normal(key_of[1], (LAYERS, D), jnp.float32), 0.5, 1.5),
        "gate_codes": with_ends(jax.random.randint(key_of[2], (LAYERS, D // 4, FF), 0, 256), jax.random.fold_in(key_of[2], 1), 0, 255).astype(jnp.int32),
        "up_codes": with_ends(jax.random.randint(key_of[3], (LAYERS, D // 4, FF), 0, 256), jax.random.fold_in(key_of[3], 1), 0, 255).astype(jnp.int32),
        "down_codes": with_ends(jax.random.randint(key_of[4], (LAYERS, FF // 4, D), 0, 256), jax.random.fold_in(key_of[4], 1), 0, 255).astype(jnp.int32),
        "gate_zero": with_ends(jax.random.randint(key_of[5], (LAYERS, D // GROUP, FF), 0, 4), jax.random.fold_in(key_of[5], 1), 0, 3).astype(jnp.int32),
        "up_zero": with_ends(jax.random.randint(key_of[6], (LAYERS, D // GROUP, FF), 0, 4), jax.random.fold_in(key_of[6], 1), 0, 3).astype(jnp.int32),
        "down_zero": with_ends(jax.random.randint(key_of[7], (LAYERS, FF // GROUP, D), 0, 4), jax.random.fold_in(key_of[7], 1), 0, 3).astype(jnp.int32),
        "gate_step": jnp.clip(jnp.exp(math.log(0.01546796) - 1.3862944 * jax.random.uniform(key_of[8], (LAYERS, D // GROUP, FF), jnp.float32) ** block_levels(key_of[8], (LAYERS, D // GROUP, FF), ((2, 32),), -0.2, 0.2)), 0.00386699, 0.01546796),
        "up_step": jnp.clip(jnp.exp(math.log(0.01546796) - 1.3862944 * jax.random.uniform(key_of[9], (LAYERS, D // GROUP, FF), jnp.float32) ** block_levels(key_of[9], (LAYERS, D // GROUP, FF), ((2, 32),), -0.2, 0.2)), 0.00386699, 0.01546796),
        "down_step": jnp.clip(jnp.exp(math.log(0.00637888) - 1.3862944 * jax.random.uniform(key_of[10], (LAYERS, FF // GROUP, D), jnp.float32) ** block_levels(key_of[10], (LAYERS, FF // GROUP, D), ((1, 32),), -0.2, 0.2)), 0.00159472, 0.00637888),
        "out_grad": normal_values(part_keys[11], (TOKENS, D), 1.0, 6.0, ((0, 32),)),
        "doc_lengths": jax.vmap(lambda own: ragged(own, DOCS, MB_TOK, MB_TOK // 2, 2))(jax.random.split(part_keys[12], MICRO)).reshape((MICRO, DOCS)).astype(jnp.int32),
    }


norm_epsilon = 1e-05

def unpack(packed):
    shifts = 2 * jnp.arange(4, dtype=jnp.int32)
    pieces = jnp.bitwise_and(jnp.right_shift(packed[:, None, :], shifts[None, :, None]), 3)
    return pieces.reshape(packed.shape[0] * 4, packed.shape[1])

def offsets_of(packed, zeros):
    return (unpack(packed) - jnp.repeat(zeros, GROUP, axis=0)).astype(jnp.float32)

def dequant(packed, zeros, steps):
    return (offsets_of(packed, zeros) * jnp.repeat(steps, GROUP, axis=0)).astype(jnp.bfloat16)

def group_grad(packed, zeros, weight_grad):
    product = offsets_of(packed, zeros) * weight_grad
    return lax.optimization_barrier(jnp.sum(product.reshape(product.shape[0] // GROUP, GROUP, product.shape[1]), axis=1))

def norm_rows(state, gain):
    values = state.astype(jnp.float32)
    scale = lax.rsqrt(lax.optimization_barrier(jnp.mean(values * values, axis=-1, keepdims=True)) + norm_epsilon)
    return (values * scale * gain).astype(jnp.bfloat16)

def norm_back(state, gain, upstream):
    values = state.astype(jnp.float32)
    scale = lax.rsqrt(lax.optimization_barrier(jnp.mean(values * values, axis=-1, keepdims=True)) + norm_epsilon)
    normal = values * scale
    inner = upstream * gain
    return scale * (inner - normal * lax.optimization_barrier(jnp.mean(inner * normal, axis=-1, keepdims=True)))

def token_lengths(doc_lengths, first_row, row_count, micro_rows):
    index_rows = first_row + jnp.arange(row_count, dtype=jnp.int32)
    batch_index = index_rows // micro_rows
    position = index_rows % micro_rows
    picked = (batch_index[:, None] == jnp.arange(doc_lengths.shape[0], dtype=jnp.int32)[None, :]).astype(jnp.int32)
    chosen = lax.optimization_barrier(jnp.sum(picked[:, :, None] * doc_lengths[None, :, :], axis=1))
    doc_ends = jnp.cumsum(chosen, axis=1)
    starts = doc_ends - chosen
    inside = (position[:, None] >= starts) & (position[:, None] < doc_ends)
    return lax.optimization_barrier(jnp.sum(jnp.where(inside, chosen, 0), axis=1)).astype(jnp.float32)

def hidden_back(cotangent, gate_pre, up_value, down_weight):
    hidden_grad = jnp.dot(cotangent, down_weight.T, preferred_element_type=jnp.float32)
    gate_sigmoid = jax.nn.sigmoid(gate_pre)
    gate_grad = (hidden_grad * up_value * gate_sigmoid * (1.0 + gate_pre * (1.0 - gate_sigmoid))).astype(jnp.bfloat16)
    up_grad = (hidden_grad * gate_pre * gate_sigmoid).astype(jnp.bfloat16)
    return (gate_grad, up_grad)

def reference(tokens, norm_gain, gate_codes, up_codes, down_codes, gate_zero, up_zero, down_zero, gate_step, up_step, down_step, out_grad, doc_lengths):
    state = tokens
    stored = []
    for layer_index in range(LAYERS):
        gate_weight = dequant(gate_codes[layer_index], gate_zero[layer_index], gate_step[layer_index])
        up_weight = dequant(up_codes[layer_index], up_zero[layer_index], up_step[layer_index])
        normed = norm_rows(state, norm_gain[layer_index])
        gate_pre = jnp.dot(normed, gate_weight, preferred_element_type=jnp.float32)
        up_value = jnp.dot(normed, up_weight, preferred_element_type=jnp.float32)
        hidden = (jax.nn.silu(gate_pre) * up_value).astype(jnp.bfloat16)
        stored.append((state, normed, gate_pre, up_value, hidden))
        if layer_index + 1 < LAYERS:
            down_weight = dequant(down_codes[layer_index], down_zero[layer_index], down_step[layer_index])
            state = (state.astype(jnp.float32) + jnp.dot(hidden, down_weight, preferred_element_type=jnp.float32)).astype(jnp.bfloat16)
    lengths_all = token_lengths(doc_lengths, 0, TOKENS, MB_TOK)
    cotangent = (out_grad.astype(jnp.float32) / lengths_all[:, None]).astype(jnp.bfloat16)
    gate_list = []
    up_list = []
    down_list = []
    for layer_index in reversed(range(LAYERS)):
        state, normed, gate_pre, up_value, hidden = stored[layer_index]
        gate_weight = dequant(gate_codes[layer_index], gate_zero[layer_index], gate_step[layer_index])
        up_weight = dequant(up_codes[layer_index], up_zero[layer_index], up_step[layer_index])
        down_weight = dequant(down_codes[layer_index], down_zero[layer_index], down_step[layer_index])
        gate_grad, up_grad = hidden_back(cotangent, gate_pre, up_value, down_weight)
        down_list.append(group_grad(down_codes[layer_index], down_zero[layer_index], jnp.dot(hidden.T, cotangent, preferred_element_type=jnp.float32)))
        gate_list.append(group_grad(gate_codes[layer_index], gate_zero[layer_index], jnp.dot(normed.T, gate_grad, preferred_element_type=jnp.float32)))
        up_list.append(group_grad(up_codes[layer_index], up_zero[layer_index], jnp.dot(normed.T, up_grad, preferred_element_type=jnp.float32)))
        normed_grad = jnp.dot(gate_grad, gate_weight.T, preferred_element_type=jnp.float32) + jnp.dot(up_grad, up_weight.T, preferred_element_type=jnp.float32)
        cotangent = (cotangent.astype(jnp.float32) + norm_back(state, norm_gain[layer_index], normed_grad)).astype(jnp.bfloat16)
    return (cotangent, jnp.stack(gate_list[::-1]), jnp.stack(up_list[::-1]), jnp.stack(down_list[::-1]))
```

```python
import jax
import jax.numpy as jnp
import numpy as np
from jax import lax
from jax.experimental import pallas as pl
from jax.experimental.pallas import tpu as pltpu
from jax.sharding import PartitionSpec as P

GROUP = 64
WORDS = GROUP // 4
LAYERS = 2
norm_epsilon = 1e-05
BF16 = jnp.bfloat16
F32 = jnp.float32


def params(mib=48):
    return pltpu.CompilerParams(vmem_limit_bytes=mib * 2**20)


def cost(flops, bytes_accessed):
    return pl.CostEstimate(flops=int(flops), bytes_accessed=int(bytes_accessed), transcendentals=0)


def block_of(size, most):
    best = size
    if size > most:
        for candidate in range(128, most + 1, 128):
            if size % candidate == 0:
                best = candidate
    return best


def dequant_kernel(code_ref, zero_ref, step_ref, out_ref, planes):
    groups, width = zero_ref.shape
    lanes = planes.shape[-1]
    for group in range(groups):
        for lane in range(0, width, lanes):
            cols = slice(lane, lane + lanes)
            words = code_ref[group * WORDS : (group + 1) * WORDS, cols]
            zero = zero_ref[group : group + 1, cols]
            step = step_ref[group : group + 1, cols]
            for piece in range(4):
                offset = ((words >> (2 * piece)) & 3) - zero
                planes[pl.ds(piece, WORDS, stride=4), :] = offset.astype(F32) * step
            out_ref[group * GROUP : (group + 1) * GROUP, cols] = planes[...].astype(BF16)


def dequant(codes, zeros, steps, layer):
    _, words, width = codes.shape
    groups = zeros.shape[1]
    if width > words:
        row_block, col_block = words, block_of(width, 1024)
    else:
        row_block, col_block = min(words, 256), width
    group_block = row_block // WORDS
    lanes = 128 if col_block % 128 == 0 else 64
    return pl.pallas_call(
        dequant_kernel,
        grid=(words // row_block, width // col_block),
        in_specs=[
            pl.BlockSpec((None, row_block, col_block), lambda i, j: (layer, i, j)),
            pl.BlockSpec((None, group_block, col_block), lambda i, j: (layer, i, j)),
            pl.BlockSpec((None, group_block, col_block), lambda i, j: (layer, i, j)),
        ],
        out_specs=pl.BlockSpec((row_block * 4, col_block), lambda i, j: (i, j)),
        out_shape=jax.ShapeDtypeStruct((words * 4, width), BF16),
        scratch_shapes=[pltpu.VMEM((GROUP, lanes), F32)],
        compiler_params=params(),
        cost_estimate=cost(words * width * 40, words * width * 12),
    )(codes, zeros, steps)


def sigmoid(value):
    return 1.0 / (1.0 + jnp.exp(-value))


def forward_kernel(x_ref, gate_ref, up_ref, gate_out, up_out, hidden_out):
    index = pl.program_id(0)
    gate = jnp.dot(x_ref[...], gate_ref[...], preferred_element_type=F32)
    up = jnp.dot(x_ref[...], up_ref[...], preferred_element_type=F32)

    @pl.when(index == 0)
    def _():
        gate_out[...] = gate
        up_out[...] = up

    @pl.when(index > 0)
    def _():
        gate_out[...] += gate
        up_out[...] += up

    @pl.when(index == pl.num_programs(0) - 1)
    def _():
        gate_all = gate_out[...]
        hidden_out[...] = (gate_all * sigmoid(gate_all) * up_out[...]).astype(BF16)


def forward(normed, gate_weight, up_weight):
    tokens, depth = normed.shape
    width = gate_weight.shape[1]
    block = block_of(depth, 1024)
    return pl.pallas_call(
        forward_kernel,
        grid=(depth // block,),
        in_specs=[
            pl.BlockSpec((tokens, block), lambda i: (0, i)),
            pl.BlockSpec((block, width), lambda i: (i, 0)),
            pl.BlockSpec((block, width), lambda i: (i, 0)),
        ],
        out_specs=[pl.BlockSpec((tokens, width), lambda i: (0, 0))] * 3,
        out_shape=[
            jax.ShapeDtypeStruct((tokens, width), F32),
            jax.ShapeDtypeStruct((tokens, width), F32),
            jax.ShapeDtypeStruct((tokens, width), BF16),
        ],
        compiler_params=params(),
        cost_estimate=cost(4 * tokens * depth * width, 4 * depth * width),
    )(normed, gate_weight, up_weight)


def rows_kernel(x_ref, weight_ref, out_ref):
    out_ref[...] = jnp.dot(x_ref[...], weight_ref[...], preferred_element_type=F32)


def rows_product(x, weight):
    tokens, depth = x.shape
    width = weight.shape[1]
    block = block_of(width, 1024)
    return pl.pallas_call(
        rows_kernel,
        grid=(width // block,),
        in_specs=[
            pl.BlockSpec((tokens, depth), lambda i: (0, 0)),
            pl.BlockSpec((depth, block), lambda i: (0, i)),
        ],
        out_specs=pl.BlockSpec((tokens, block), lambda i: (0, i)),
        out_shape=jax.ShapeDtypeStruct((tokens, width), F32),
        compiler_params=params(),
        cost_estimate=cost(2 * tokens * depth * width, 2 * depth * width),
    )(x, weight)


def across(left, right):
    return lax.dot_general(left, right, (((1,), (1,)), ((), ())), preferred_element_type=F32)


def hidden_grad_kernel(cot_ref, weight_ref, out_ref):
    part = across(cot_ref[...], weight_ref[...])

    @pl.when(pl.program_id(0) == 0)
    def _():
        out_ref[...] = part

    @pl.when(pl.program_id(0) > 0)
    def _():
        out_ref[...] += part


def hidden_grad_of(cot, weight):
    tokens, width = cot.shape
    depth = weight.shape[0]
    block = block_of(width, 1024)
    return pl.pallas_call(
        hidden_grad_kernel,
        grid=(width // block,),
        in_specs=[
            pl.BlockSpec((tokens, block), lambda i: (0, i)),
            pl.BlockSpec((depth, block), lambda i: (0, i)),
        ],
        out_specs=pl.BlockSpec((tokens, depth), lambda i: (0, 0)),
        out_shape=jax.ShapeDtypeStruct((tokens, depth), F32),
        compiler_params=params(),
        cost_estimate=cost(2 * tokens * depth * width, 2 * depth * width),
    )(cot, weight)


def normed_grad_kernel(gate_grad_ref, up_grad_ref, gate_ref, up_ref, out_ref):
    out_ref[...] = across(gate_grad_ref[...], gate_ref[...]) + across(up_grad_ref[...], up_ref[...])


def normed_grad_of(gate_grad, up_grad, gate_weight, up_weight):
    tokens, width = gate_grad.shape
    depth = gate_weight.shape[0]
    block = block_of(depth, 1024)
    return pl.pallas_call(
        normed_grad_kernel,
        grid=(depth // block,),
        in_specs=[
            pl.BlockSpec((tokens, width), lambda i: (0, 0)),
            pl.BlockSpec((tokens, width), lambda i: (0, 0)),
            pl.BlockSpec((block, width), lambda i: (i, 0)),
            pl.BlockSpec((block, width), lambda i: (i, 0)),
        ],
        out_specs=pl.BlockSpec((tokens, block), lambda i: (0, i)),
        out_shape=jax.ShapeDtypeStruct((tokens, depth), F32),
        compiler_params=params(),
        cost_estimate=cost(4 * tokens * depth * width, 4 * depth * width),
    )(gate_grad, up_grad, gate_weight, up_weight)


def spread(x, groups):
    tokens, columns = x.shape
    tall = jnp.concatenate([x] * groups, axis=0)
    row_group = lax.broadcasted_iota(jnp.int32, tall.shape, 0) // tokens
    col_group = lax.broadcasted_iota(jnp.int32, tall.shape, 1) // GROUP
    return jnp.where(row_group == col_group, tall.astype(F32), 0.0).astype(BF16)


def step_grad_block(x, weight, upstream, step):
    tokens = x.shape[0]
    rows = []
    groups = weight.shape[0] // GROUP
    for first in range(0, groups, 4):
        count = min(4, groups - first)
        part = slice(first * GROUP, (first + count) * GROUP)
        product = jnp.dot(spread(x[:, part], count), weight[part, :], preferred_element_type=F32)
        for group in range(count):
            own = product[group * tokens : (group + 1) * tokens] * upstream
            rows.append(jnp.sum(own, axis=0, keepdims=True))
    return jnp.concatenate(rows, axis=0) / step


def step_grad_kernel(x_ref, weight_ref, upstream_ref, step_ref, *refs):
    refs[-1][...] = step_grad_block(
        x_ref[...], weight_ref[...], upstream_ref[...].astype(F32), step_ref[...]
    )


def step_grad(x, weight, upstream, steps, layer, earlier):
    tokens, depth = x.shape
    width = weight.shape[1]
    if width > depth:
        row_block, col_block = depth, block_of(width, 1024)
    else:
        row_block, col_block = block_of(depth, 1024), width
    group_block = row_block // GROUP
    operands = [x, weight, upstream, steps]
    in_specs = [
        pl.BlockSpec((tokens, row_block), lambda i, j: (0, i)),
        pl.BlockSpec((row_block, col_block), lambda i, j: (i, j)),
        pl.BlockSpec((tokens, col_block), lambda i, j: (0, j)),
        pl.BlockSpec((None, group_block, col_block), lambda i, j: (layer, i, j)),
    ]
    aliases = {}
    if earlier is not None:
        operands.append(earlier)
        in_specs.append(pl.BlockSpec(memory_space=pl.ANY))
        aliases = {4: 0}
    return pl.pallas_call(
        step_grad_kernel,
        grid=(depth // row_block, width // col_block),
        in_specs=in_specs,
        out_specs=pl.BlockSpec((None, group_block, col_block), lambda i, j: (layer, i, j)),
        out_shape=jax.ShapeDtypeStruct(steps.shape, F32),
        input_output_aliases=aliases,
        compiler_params=params(),
        cost_estimate=cost(8 * tokens * depth * width, 2 * depth * width),
    )(*operands)


def swap(value, bit):
    count = lax.axis_size("tensor")
    return lax.ppermute(value, "tensor", [(i, i ^ bit) for i in range(count)])


def own_bit(bit):
    return (lax.axis_index("tensor") // bit) % 2


def halve(value, bit, axis=0):
    half = value.shape[axis] // 2
    mine = own_bit(bit)
    kept = lax.dynamic_slice_in_dim(value, mine * half, half, axis)
    sent = lax.dynamic_slice_in_dim(value, (1 - mine) * half, half, axis)
    got = swap(sent.astype(BF16), bit)
    return kept.astype(F32) + got.astype(F32)


def add_up(value, bit):
    rounded = value.astype(BF16)
    return rounded.astype(F32) + swap(rounded, bit).astype(F32)


def double(value, bit, axis):
    other = swap(value, bit)
    mine = own_bit(bit) == 0
    return jnp.concatenate(
        [jnp.where(mine, value, other), jnp.where(mine, other, value)], axis=axis
    )


def inverse_rms(values):
    return lax.rsqrt(jnp.mean(values * values, axis=-1, keepdims=True) + norm_epsilon)


def norm_rows(state, gain):
    values = state.astype(F32)
    return (values * inverse_rms(values) * gain).astype(BF16)


def norm_back(state, gain, upstream):
    values = state.astype(F32)
    scale = inverse_rms(values)
    normal = values * scale
    inner = upstream * gain
    return scale * (inner - normal * jnp.mean(inner * normal, axis=-1, keepdims=True))


def token_lengths(doc_lengths, index_rows, micro_rows):
    batch_index = index_rows // micro_rows
    position = index_rows % micro_rows
    picked = batch_index[:, None] == jnp.arange(doc_lengths.shape[0], dtype=jnp.int32)[None, :]
    chosen = jnp.sum(jnp.where(picked[:, :, None], doc_lengths[None, :, :], 0), axis=1)
    ends = jnp.sum(
        jnp.where(
            jnp.arange(chosen.shape[1])[:, None] <= jnp.arange(chosen.shape[1])[None, :],
            chosen[:, :, None],
            0,
        ),
        axis=1,
    )
    starts = ends - chosen
    inside = (position[:, None] >= starts) & (position[:, None] < ends)
    return jnp.sum(jnp.where(inside, chosen, 0), axis=1).astype(F32)


def hidden_back(hidden_grad, gate_pre, up_value):
    gate_sigmoid = sigmoid(gate_pre)
    gate_grad = (
        hidden_grad * up_value * gate_sigmoid * (1.0 + gate_pre * (1.0 - gate_sigmoid))
    ).astype(BF16)
    up_grad = (hidden_grad * gate_pre * gate_sigmoid).astype(BF16)
    return gate_grad, up_grad


def on_device(
    tokens,
    norm_gain,
    gate_codes,
    up_codes,
    down_codes,
    gate_zero,
    up_zero,
    down_zero,
    gate_step,
    up_step,
    down_step,
    out_grad,
    doc_lengths,
):
    shard_rows, features = tokens.shape
    device_count = lax.axis_size("tensor")
    micro_rows = shard_rows * device_count // doc_lengths.shape[0]
    bits = [1 << k for k in range(device_count.bit_length() - 1)]
    near, far = bits[:-2], bits[-2:]

    far_count = 1 << len(far)
    far_index = np.arange(far_count)
    far_place = sum(((far_index >> k) & 1) << (len(far) - 1 - k) for k in range(len(far)))
    far_device = np.argsort(far_place)
    near_part = lax.axis_index("tensor") % (1 << len(near))
    device_ids = near_part + jnp.asarray(far_device << len(near), jnp.int32)
    row_ids = (
        device_ids[:, None] * shard_rows + jnp.arange(shard_rows, dtype=jnp.int32)[None, :]
    ).reshape(-1)
    lengths = token_lengths(doc_lengths, row_ids, micro_rows)

    weights = []
    for layer in range(LAYERS):
        weights.append(
            (
                dequant(gate_codes, gate_zero, gate_step, layer),
                dequant(up_codes, up_zero, up_step, layer),
                dequant(down_codes, down_zero, down_step, layer),
            )
        )

    pair = jnp.stack([tokens, out_grad])
    for bit in reversed(far):
        pair = double(pair, bit, 1)
    state_rows = [pair[0]]
    cot_rows = (pair[1].astype(F32) / lengths[:, None]).astype(BF16)
    pair = jnp.stack([norm_rows(pair[0], norm_gain[0]), cot_rows])
    for bit in reversed(near):
        pair = double(pair, bit, 1)
    normed, cotangent = pair[0], pair[1]

    stored = []
    for layer in range(LAYERS):
        gate_weight, up_weight, down_weight = weights[layer]
        gate_pre, up_value, hidden = forward(normed, gate_weight, up_weight)
        stored.append((normed, gate_pre, up_value, hidden))
        if layer + 1 < LAYERS:
            part = rows_product(hidden, down_weight)
            for bit in near:
                part = halve(part, bit)
            for bit in far:
                part = add_up(part, bit)
            state_rows.append((state_rows[layer].astype(F32) + part).astype(BF16))
            normed = norm_rows(state_rows[-1], norm_gain[layer + 1])
            for bit in reversed(near):
                normed = double(normed, bit, 0)

    gate_out = up_out = down_out = None
    result = None
    for layer in reversed(range(LAYERS)):
        normed, gate_pre, up_value, hidden = stored[layer]
        gate_weight, up_weight, down_weight = weights[layer]
        hidden_grad = hidden_grad_of(cotangent, down_weight)
        gate_grad, up_grad = hidden_back(hidden_grad, gate_pre, up_value)
        part = normed_grad_of(gate_grad, up_grad, gate_weight, up_weight)
        down_out = step_grad(hidden, down_weight, cotangent, down_step, layer, down_out)
        gate_out = step_grad(normed, gate_weight, gate_grad, gate_step, layer, gate_out)
        up_out = step_grad(normed, up_weight, up_grad, up_step, layer, up_out)
        for bit in near:
            part = halve(part, bit)
        if layer > 0:
            for bit in far:
                part = add_up(part, bit)
            cot_rows = (
                cot_rows.astype(F32) + norm_back(state_rows[layer], norm_gain[layer], part)
            ).astype(BF16)
            cotangent = cot_rows
            for bit in reversed(near):
                cotangent = double(cotangent, bit, 0)
        else:
            own_cot = cot_rows
            for bit in far:
                part = halve(part, bit)
                half = own_cot.shape[0] // 2
                own_cot = lax.dynamic_slice_in_dim(own_cot, own_bit(bit) * half, half, 0)
            result = (
                own_cot.astype(F32) + norm_back(tokens, norm_gain[0], part)
            ).astype(BF16)
    return result, gate_out, up_out, down_out


def solution(mesh):
    placed = (
        P(("groups", "tensor"), None),
        P(),
        P(None, None, "tensor"),
        P(None, None, "tensor"),
        P(None, "tensor", None),
        P(None, None, "tensor"),
        P(None, None, "tensor"),
        P(None, "tensor", None),
        P(None, None, "tensor"),
        P(None, None, "tensor"),
        P(None, "tensor", None),
        P(("groups", "tensor"), None),
        P("groups", None),
    )
    return jax.shard_map(
        on_device,
        mesh=mesh,
        in_specs=placed,
        out_specs=(
            P(("groups", "tensor"), None),
            P("groups", None, "tensor"),
            P("groups", None, "tensor"),
            P("groups", "tensor", None),
        ),
        check_vma=False,
    )
```

```python
import functools

import jax
import jax.numpy as jnp
import numpy as np
from jax import lax
from jax.experimental import pallas as pl
from jax.experimental.pallas import tpu as pltpu
from jax.sharding import PartitionSpec as P

GROUP = 64
WORDS = GROUP // 4
LAYERS = 2
norm_epsilon = 1e-05
BF16 = jnp.bfloat16
F32 = jnp.float32
OFFSET = jnp.float8_e4m3fn
ANYWHERE = pl.BlockSpec(memory_space=pl.ANY)
IN_HBM = pl.BlockSpec(memory_space=pltpu.HBM)


def params(mib=60):
    return pltpu.CompilerParams(vmem_limit_bytes=mib * 2**20)


def cost(flops, bytes_accessed):
    return pl.CostEstimate(flops=int(flops), bytes_accessed=int(bytes_accessed), transcendentals=0)


def block_of(size, most):
    best = size
    if size > most:
        for candidate in range(128, most + 1, 128):
            if size % candidate == 0:
                best = candidate
    return best


def copy_in(source, target, sem):
    copy = pltpu.make_async_copy(source, target, sem)
    copy.start()
    return copy


def row_chunk(chunk, size):
    return pl.ds(pl.multiple_of(chunk * size, size), size)


def one_row(ref, row, cols):
    if len(ref.shape) == 2:
        return ref[row : row + 1, cols]
    held = ref.shape[1]
    return ref[row // held, row % held : row % held + 1, cols]


COUNT = 8
AHEAD = 2


def stream(count, copies, work, before=None, last=None):
    for chunk in range(AHEAD):
        for copy in copies(chunk):
            copy.start()
    if before is not None:
        before()

    def step(chunk, _):
        for copy in copies(chunk):
            copy.wait()

        @pl.when(chunk + AHEAD < count)
        def _():
            for copy in copies(chunk + AHEAD):
                copy.start()

        if last is not None:
            @pl.when(chunk + AHEAD >= count)
            def _():
                last(chunk + AHEAD - count)

        work(chunk)
        return 0

    lax.fori_loop(0, count, step, 0)


def offsets_kernel(layer, along_rows, count, code_any, zero_any, out_any, code, zero, out, planes, sems):
    words, width = code.shape
    rows = words // count if along_rows else words
    lanes = width if along_rows else width // count
    tile = planes.shape[-1]
    slots = planes.shape[0]

    def code_part(chunk):
        if along_rows:
            return (row_chunk(chunk, rows), slice(None))
        return (slice(None), row_chunk(chunk, lanes))

    def out_part(chunk):
        if along_rows:
            return (row_chunk(chunk, rows * 4), slice(None))
        return (slice(None), row_chunk(chunk, lanes))

    def code_copy(chunk):
        part = code_part(chunk)
        return pltpu.make_async_copy(code_any.at[(layer,) + part], code.at[part], sems.at[chunk])

    def out_copy(chunk):
        part = out_part(chunk)
        return pltpu.make_async_copy(out.at[part], out_any.at[part], sems.at[count + chunk])

    zero_copy = pltpu.make_async_copy(zero_any.at[layer], zero, sems.at[2 * count])
    zero_copy.start()
    groups = rows // WORDS

    def work(chunk):
        def unit(held, zeros, place, cols, slot):
            for piece in range(4):
                offset = ((held >> (2 * piece)) & 3) - zeros
                planes[slot, pl.ds(piece, WORDS, stride=4), :] = offset.astype(F32)
            out[place, cols] = planes[slot].astype(OFFSET)

        if along_rows:

            def some_groups(block, _):
                first = chunk * groups + block * 8
                for index in range(width // tile):
                    cols = slice(index * tile, (index + 1) * tile)
                    zeros = zero[row_chunk(first // 8, 8), cols]
                    for group in range(8):
                        held = code[row_chunk(first + group, WORDS), cols]
                        place = row_chunk(first + group, GROUP)
                        unit(held, zeros[group : group + 1], place, cols, group)
                return 0

            lax.fori_loop(0, groups // 8, some_groups, 0)
        else:

            def some_lanes(index, _):
                cols = pl.ds(pl.multiple_of(chunk * lanes + index * tile, tile), tile)
                for group in range(groups):
                    held = code[group * WORDS : (group + 1) * WORDS, cols]
                    place = slice(group * GROUP, (group + 1) * GROUP)
                    unit(held, one_row(zero, group, cols), place, cols, group % slots)
                return 0

            lax.fori_loop(0, lanes // tile, some_lanes, 0)
        out_copy(chunk).start()

    stream(count, lambda chunk: [code_copy(chunk)], work, zero_copy.wait)
    for chunk in range(count):
        out_copy(chunk).wait()


def offsets_of(codes, zeros, layer):
    _, words, width = codes.shape
    along_rows = words >= width
    tile = 128 if width % 128 == 0 else 64
    count = COUNT
    return pl.pallas_call(
        functools.partial(offsets_kernel, layer, along_rows, count),
        in_specs=[IN_HBM, IN_HBM],
        out_specs=IN_HBM,
        out_shape=jax.ShapeDtypeStruct((words * 4, width), OFFSET),
        scratch_shapes=[
            pltpu.VMEM((words, width), jnp.int32),
            pltpu.VMEM(zeros.shape[1:], jnp.int32),
            pltpu.VMEM((words * 4, width), OFFSET),
            pltpu.VMEM((8, GROUP, tile), F32),
            pltpu.SemaphoreType.DMA((2 * count + 1,)),
        ],
        compiler_params=params(),
        cost_estimate=cost(words * width * 40, words * width * 8),
    )(codes, zeros)


def sigmoid(value):
    return 1.0 / (1.0 + jnp.exp(-value))


def across(left, right):
    return lax.dot_general(left, right, (((1,), (1,)), ((), ())), preferred_element_type=F32)


def weights_of(offsets, steps):
    parts = []
    for group, step in enumerate(steps):
        part = offsets[group * GROUP : (group + 1) * GROUP].astype(F32)
        parts.append((part * step).astype(BF16))
    return jnp.concatenate(parts, axis=0)


class Matrix:
    def __init__(self, layer, source, step_source, offsets, steps, sems, by_rows):
        self.layer, self.source, self.step_source = layer, source, step_source
        self.offsets, self.steps, self.sems, self.by_rows = offsets, steps, sems, by_rows
        self.count = COUNT
        self.size = offsets.shape[0 if by_rows else 1] // self.count

    def part(self, chunk):
        if self.by_rows:
            return (row_chunk(chunk, self.size), slice(None))
        return (slice(None), row_chunk(chunk, self.size))

    def step_copy(self):
        return pltpu.make_async_copy(
            self.step_source.at[self.layer], self.steps, self.sems.at[self.count]
        )

    def copy(self, chunk):
        part = self.part(chunk)
        return pltpu.make_async_copy(self.source.at[part], self.offsets.at[part], self.sems.at[chunk])

    def weights(self, chunk):
        offsets = self.offsets[self.part(chunk)]
        groups = offsets.shape[0] // GROUP
        if self.by_rows:
            held = self.steps[row_chunk(chunk, groups), :]
            steps = [held[group : group + 1] for group in range(groups)]
        else:
            cols = row_chunk(chunk, self.size)
            steps = [one_row(self.steps, group, cols) for group in range(groups)]
        return weights_of(offsets, steps)

    @staticmethod
    def scratch(offsets, steps):
        return [
            pltpu.VMEM(offsets.shape, OFFSET),
            pltpu.VMEM(steps.shape[1:], F32),
            pltpu.SemaphoreType.DMA((COUNT + 1,)),
        ]


def gate_up_forward(x, gate, up, gate_out, up_out, before, last=None):
    def work(chunk):
        rows = x[:, row_chunk(chunk, gate.size)]
        gate_out[...] += jnp.dot(rows, gate.weights(chunk), preferred_element_type=F32)
        up_out[...] += jnp.dot(rows, up.weights(chunk), preferred_element_type=F32)

    def ready():
        gate_out[...] = jnp.zeros_like(gate_out)
        up_out[...] = jnp.zeros_like(up_out)
        before()
        gate.step_copy().wait()
        up.step_copy().wait()

    gate.step_copy().start()
    up.step_copy().start()
    stream(gate.count, lambda chunk: [gate.copy(chunk), up.copy(chunk)], work, ready, last)
    gate_all = gate_out[...]
    return (gate_all * sigmoid(gate_all) * up_out[...]).astype(BF16)


def hidden_back(hidden_grad, gate_pre, up_value):
    gate_sigmoid = sigmoid(gate_pre)
    gate_grad = (
        hidden_grad * up_value * gate_sigmoid * (1.0 + gate_pre * (1.0 - gate_sigmoid))
    ).astype(BF16)
    up_grad = (hidden_grad * gate_pre * gate_sigmoid).astype(BF16)
    return gate_grad, up_grad


def gate_up_backward(gate_grad, up_grad, gate, up, out, chunk):
    part = across(gate_grad, gate.weights(chunk)) + across(up_grad, up.weights(chunk))
    out[:, row_chunk(chunk, gate.size)] = part.astype(BF16)


def cot_down(cot, down, out, before, last=None):
    def work(chunk):
        out[...] += across(cot[:, row_chunk(chunk, down.size)], down.weights(chunk))

    def ready():
        out[...] = jnp.zeros_like(out)
        before()
        down.step_copy().wait()

    down.step_copy().start()
    stream(down.count, lambda chunk: [down.copy(chunk)], work, ready, last)


def later(count, copies, work):
    def step(chunk, _):
        for copy in copies(chunk):
            copy.wait()

        @pl.when(chunk + AHEAD < count)
        def _():
            for copy in copies(chunk + AHEAD):
                copy.start()

        work(chunk)
        return 0

    lax.fori_loop(0, count, step, 0)


def first_forward_kernel(layer, x_any, gate_any, up_any, down_any, gs_any, us_any, ds_any, *refs):
    gate_out, up_out, hidden_out, part_out = refs[:4]
    x, sem = refs[4:6]
    gate = Matrix(layer, gate_any, gs_any, *refs[6:9], True)
    up = Matrix(layer, up_any, us_any, *refs[9:12], True)
    down = Matrix(layer, down_any, ds_any, *refs[12:15], False)
    x_copy = copy_in(x_any, x, sem.at[0])

    def last(chunk):
        down.copy(chunk).start()

    hidden = gate_up_forward(x, gate, up, gate_out, up_out, x_copy.wait, last)
    down.step_copy().start()
    hidden_out[...] = hidden
    down.step_copy().wait()

    def work(chunk):
        part = jnp.dot(hidden_out[...], down.weights(chunk), preferred_element_type=F32)
        part_out[:, row_chunk(chunk, down.size)] = part.astype(BF16)

    later(down.count, lambda chunk: [down.copy(chunk)], work)


def first_forward(layer, x, gate, up, down, gate_step, up_step, down_step):
    tokens, depth = x.shape
    width = gate.shape[1]
    return pl.pallas_call(
        functools.partial(first_forward_kernel, layer),
        in_specs=[ANYWHERE] + [IN_HBM] * 6,
        out_shape=[
            jax.ShapeDtypeStruct((tokens, width), F32),
            jax.ShapeDtypeStruct((tokens, width), F32),
            jax.ShapeDtypeStruct((tokens, width), BF16),
            jax.ShapeDtypeStruct((tokens, depth), BF16),
        ],
        scratch_shapes=[pltpu.VMEM(x.shape, BF16), pltpu.SemaphoreType.DMA((1,))]
        + Matrix.scratch(gate, gate_step)
        + Matrix.scratch(up, up_step)
        + Matrix.scratch(down, down_step),
        compiler_params=params(),
        cost_estimate=cost(6 * tokens * depth * width, 3 * depth * width),
    )(x, gate, up, down, gate_step, up_step, down_step)


def hidden_grad_kernel(layer, cot_any, down_any, ds_any, out, cot, sem, *refs):
    down = Matrix(layer, down_any, ds_any, *refs, False)
    cot_copy = copy_in(cot_any, cot, sem.at[0])
    cot_down(cot, down, out, cot_copy.wait)


def hidden_grad_of(layer, cot, down, down_step):
    tokens, features = cot.shape
    return pl.pallas_call(
        functools.partial(hidden_grad_kernel, layer),
        in_specs=[ANYWHERE] + [IN_HBM] * 2,
        out_shape=jax.ShapeDtypeStruct((tokens, down.shape[0]), F32),
        scratch_shapes=[pltpu.VMEM(cot.shape, BF16), pltpu.SemaphoreType.DMA((1,))]
        + Matrix.scratch(down, down_step),
        compiler_params=params(),
        cost_estimate=cost(2 * tokens * features * down.shape[0], features * down.shape[0]),
    )(cot, down, down_step)


def last_layer_kernel(layer, x_any, grad_any, gate_any, up_any, gs_any, us_any, *refs):
    hidden_out, gate_grad_out, up_grad_out, part_out = refs[:4]
    gate_pre, up_value, x, hidden_grad, sem = refs[4:9]
    gate = Matrix(layer, gate_any, gs_any, *refs[9:12], True)
    up = Matrix(layer, up_any, us_any, *refs[12:15], True)
    x_copy = copy_in(x_any, x, sem.at[0])
    grad_copy = copy_in(grad_any, hidden_grad, sem.at[1])
    hidden_out[...] = gate_up_forward(x, gate, up, gate_pre, up_value, x_copy.wait)
    grad_copy.wait()
    gate_grad, up_grad = hidden_back(hidden_grad[...], gate_pre[...], up_value[...])
    gate_grad_out[...] = gate_grad
    up_grad_out[...] = up_grad

    def work(chunk, _):
        gate_up_backward(gate_grad_out[...], up_grad_out[...], gate, up, part_out, chunk)
        return 0

    lax.fori_loop(0, gate.count, work, 0)


def last_layer(layer, x, hidden_grad, gate, up, gate_step, up_step):
    tokens, depth = x.shape
    width = gate.shape[1]
    small = jax.ShapeDtypeStruct((tokens, width), BF16)
    return pl.pallas_call(
        functools.partial(last_layer_kernel, layer),
        in_specs=[ANYWHERE] * 2 + [IN_HBM] * 4,
        out_shape=[small, small, small, jax.ShapeDtypeStruct((tokens, depth), BF16)],
        scratch_shapes=[
            pltpu.VMEM((tokens, width), F32),
            pltpu.VMEM((tokens, width), F32),
            pltpu.VMEM(x.shape, BF16),
            pltpu.VMEM((tokens, width), F32),
            pltpu.SemaphoreType.DMA((2,)),
        ]
        + Matrix.scratch(gate, gate_step)
        + Matrix.scratch(up, up_step),
        compiler_params=params(),
        cost_estimate=cost(8 * tokens * depth * width, 2 * depth * width),
    )(x, hidden_grad, gate, up, gate_step, up_step)


def backward_kernel(layer, cot_any, pre_any, value_any, gate_any, up_any, down_any, gs_any, us_any, ds_any, *refs):
    gate_grad_out, up_grad_out, part_out = refs[:3]
    cot, gate_pre, up_value, hidden_grad, sem = refs[3:8]
    gate = Matrix(layer, gate_any, gs_any, *refs[8:11], True)
    up = Matrix(layer, up_any, us_any, *refs[11:14], True)
    down = Matrix(layer, down_any, ds_any, *refs[14:17], False)
    cot_copy = copy_in(cot_any, cot, sem.at[0])
    pre_copy = copy_in(pre_any, gate_pre, sem.at[1])
    value_copy = copy_in(value_any, up_value, sem.at[2])

    def last(chunk):
        gate.copy(chunk).start()
        up.copy(chunk).start()

    cot_down(cot, down, hidden_grad, cot_copy.wait, last)
    gate.step_copy().start()
    up.step_copy().start()
    pre_copy.wait()
    value_copy.wait()
    gate_grad, up_grad = hidden_back(hidden_grad[...], gate_pre[...], up_value[...])
    gate_grad_out[...] = gate_grad
    up_grad_out[...] = up_grad
    gate.step_copy().wait()
    up.step_copy().wait()

    def work(chunk):
        gate_up_backward(gate_grad_out[...], up_grad_out[...], gate, up, part_out, chunk)

    later(gate.count, lambda chunk: [gate.copy(chunk), up.copy(chunk)], work)


def backward(layer, cot, gate_pre, up_value, gate, up, down, gate_step, up_step, down_step):
    tokens, depth = cot.shape
    width = gate.shape[1]
    small = jax.ShapeDtypeStruct((tokens, width), BF16)
    return pl.pallas_call(
        functools.partial(backward_kernel, layer),
        in_specs=[ANYWHERE] * 3 + [IN_HBM] * 6,
        out_shape=[small, small, jax.ShapeDtypeStruct((tokens, depth), BF16)],
        scratch_shapes=[
            pltpu.VMEM(cot.shape, BF16),
            pltpu.VMEM((tokens, width), F32),
            pltpu.VMEM((tokens, width), F32),
            pltpu.VMEM((tokens, width), F32),
            pltpu.SemaphoreType.DMA((3,)),
        ]
        + Matrix.scratch(gate, gate_step)
        + Matrix.scratch(up, up_step)
        + Matrix.scratch(down, down_step),
        compiler_params=params(),
        cost_estimate=cost(6 * tokens * depth * width, 3 * depth * width),
    )(cot, gate_pre, up_value, gate, up, down, gate_step, up_step, down_step)


def spread(x, groups):
    tokens = x.shape[0]
    tall = jnp.concatenate([x] * groups, axis=0)
    row_group = lax.broadcasted_iota(jnp.int32, tall.shape, 0) // tokens
    col_group = lax.broadcasted_iota(jnp.int32, tall.shape, 1) // GROUP
    return jnp.where(row_group == col_group, tall.astype(F32), 0.0).astype(BF16)


def step_grad_block(x, offsets, upstream):
    tokens = x.shape[0]
    rows = []
    groups = offsets.shape[0] // GROUP
    for first in range(0, groups, 4):
        count = min(4, groups - first)
        part = slice(first * GROUP, (first + count) * GROUP)
        product = jnp.dot(
            spread(x[:, part], count), offsets[part, :].astype(BF16), preferred_element_type=F32
        )
        for group in range(count):
            own = product[group * tokens : (group + 1) * tokens] * upstream
            rows.append(jnp.sum(own, axis=0, keepdims=True))
    return jnp.concatenate(rows, axis=0)


def step_grad_kernel(by_rows, x_any, off_any, grad_any, *refs):
    out, x, offsets, grad, sem, sems = refs[-6:]
    count = sems.shape[0]
    size = offsets.shape[0 if by_rows else 1] // count

    def copy(chunk):
        part = (row_chunk(chunk, size), slice(None)) if by_rows else (slice(None), row_chunk(chunk, size))
        return pltpu.make_async_copy(off_any.at[part], offsets.at[part], sems.at[chunk])

    x_copy = copy_in(x_any, x, sem.at[0])
    grad_copy = copy_in(grad_any, grad, sem.at[1])
    def ready():
        x_copy.wait()
        grad_copy.wait()

    def work(chunk):
        part = row_chunk(chunk, size)
        if by_rows:
            out[row_chunk(chunk, size // GROUP), :] = step_grad_block(
                x[:, part], offsets[part, :], grad[...].astype(F32)
            )
        else:
            found = step_grad_block(x[...], offsets[:, part], grad[:, part].astype(F32))
            held = out.shape[1]
            for place in range(out.shape[0]):
                out[place, :, part] = found[place * held : (place + 1) * held]

    stream(count, lambda chunk: [copy(chunk)], work, ready)


def step_grad(x, offsets, upstream, shape, layer, earlier):
    tokens, depth = x.shape
    width = offsets.shape[1]
    by_rows = depth >= width
    operands = [x, offsets, upstream]
    aliases = {}
    if earlier is not None:
        operands.append(earlier)
        aliases = {3: 0}
    return pl.pallas_call(
        functools.partial(step_grad_kernel, by_rows),
        grid=(1,),
        in_specs=[ANYWHERE, IN_HBM, ANYWHERE, IN_HBM][: len(operands)],
        out_specs=pl.BlockSpec((None,) + shape[1:], lambda i: (layer,) + (0,) * (len(shape) - 1)),
        out_shape=jax.ShapeDtypeStruct(shape, F32),
        scratch_shapes=[
            pltpu.VMEM(x.shape, BF16),
            pltpu.VMEM(offsets.shape, OFFSET),
            pltpu.VMEM(upstream.shape, BF16),
            pltpu.SemaphoreType.DMA((2,)),
            pltpu.SemaphoreType.DMA((COUNT,)),
        ],
        input_output_aliases=aliases,
        compiler_params=params(),
        cost_estimate=cost(8 * tokens * depth * width, depth * width),
    )(*operands)


class Side:
    def __init__(self):
        self.jobs = []

    def add(self, call, *operands):
        job = [call, operands, None]
        self.jobs.append(job)
        return job

    def skip(self):
        self.jobs.append(None)

    def swap(self, value, bit):
        count = lax.axis_size("tensor")
        pairs = [(i, i ^ bit) for i in range(count)]
        job = self.jobs.pop(0) if self.jobs else None
        if job is None:
            return lax.ppermute(value, "tensor", pairs)
        value, operands = lax.optimization_barrier((value, job[1]))
        got = lax.ppermute(value, "tensor", pairs)
        got, job[2] = lax.optimization_barrier((got, job[0](*operands)))
        return got

    def finish(self):
        for job in self.jobs:
            if job is not None:
                job[2] = job[0](*job[1])
        self.jobs = []


def own_bit(bit):
    return (lax.axis_index("tensor") // bit) % 2


def halve(side, value, bit):
    half = value.shape[0] // 2
    mine = own_bit(bit)
    kept = lax.dynamic_slice_in_dim(value, mine * half, half, 0)
    sent = lax.dynamic_slice_in_dim(value, (1 - mine) * half, half, 0)
    got = side.swap(sent.astype(BF16), bit)
    return kept.astype(F32) + got.astype(F32)


def add_up(side, value, bit):
    rounded = value.astype(BF16)
    return rounded.astype(F32) + side.swap(rounded, bit).astype(F32)


def double(side, value, bit, axis):
    other = side.swap(value, bit)
    mine = own_bit(bit) == 0
    return jnp.concatenate(
        [jnp.where(mine, value, other), jnp.where(mine, other, value)], axis=axis
    )


def inverse_rms(values):
    return lax.rsqrt(jnp.mean(values * values, axis=-1, keepdims=True) + norm_epsilon)


def norm_rows(state, gain):
    values = state.astype(F32)
    return (values * inverse_rms(values) * gain).astype(BF16)


def norm_back(state, gain, upstream):
    values = state.astype(F32)
    scale = inverse_rms(values)
    normal = values * scale
    inner = upstream * gain
    return scale * (inner - normal * jnp.mean(inner * normal, axis=-1, keepdims=True))


def token_lengths(doc_lengths, index_rows, micro_rows):
    batch_index = index_rows // micro_rows
    position = index_rows % micro_rows
    picked = batch_index[:, None] == jnp.arange(doc_lengths.shape[0], dtype=jnp.int32)[None, :]
    chosen = jnp.sum(jnp.where(picked[:, :, None], doc_lengths[None, :, :], 0), axis=1)
    ends = jnp.sum(
        jnp.where(
            jnp.arange(chosen.shape[1])[:, None] <= jnp.arange(chosen.shape[1])[None, :],
            chosen[:, :, None],
            0,
        ),
        axis=1,
    )
    starts = ends - chosen
    inside = (position[:, None] >= starts) & (position[:, None] < ends)
    return jnp.sum(jnp.where(inside, chosen, 0), axis=1).astype(F32)


def on_device(
    tokens,
    norm_gain,
    gate_codes,
    up_codes,
    down_codes,
    gate_zero,
    up_zero,
    down_zero,
    gate_step,
    up_step,
    down_step,
    out_grad,
    doc_lengths,
):
    shard_rows, features = tokens.shape
    device_count = lax.axis_size("tensor")
    micro_rows = shard_rows * device_count // doc_lengths.shape[0]
    bits = [1 << k for k in range(device_count.bit_length() - 1)]
    near, far = bits[:-2], bits[-2:]

    far_count = 1 << len(far)
    far_index = np.arange(far_count)
    far_place = sum(((far_index >> k) & 1) << (len(far) - 1 - k) for k in range(len(far)))
    far_device = np.argsort(far_place)
    near_part = lax.axis_index("tensor") % (1 << len(near))
    device_ids = near_part + jnp.asarray(far_device << len(near), jnp.int32)
    row_ids = (
        device_ids[:, None] * shard_rows + jnp.arange(shard_rows, dtype=jnp.int32)[None, :]
    ).reshape(-1)
    lengths = token_lengths(doc_lengths, row_ids, micro_rows)

    down_shape = down_step.shape
    held = 4 if down_shape[1] % 4 == 0 else down_shape[1]
    tiled = (down_shape[0], down_shape[1] // held, held, down_shape[2])
    down_step, down_zero = down_step.reshape(tiled), down_zero.reshape(tiled)

    def offsets_job(side, codes, zeros, layer):
        return side.add(lambda c, z: offsets_of(c, z, layer), codes, zeros)

    side = Side()
    gate_job = offsets_job(side, gate_codes, gate_zero, 0)
    up_job = offsets_job(side, up_codes, up_zero, 0)
    down_job = offsets_job(side, down_codes, down_zero, 0)
    pair = jnp.stack([tokens, out_grad])
    for bit in reversed(far):
        pair = double(side, pair, bit, 1)
    state_0 = pair[0]
    cot_rows = (pair[1].astype(F32) / lengths[:, None]).astype(BF16)
    pair = jnp.stack([norm_rows(state_0, norm_gain[0]), cot_rows])
    for bit in reversed(near):
        pair = double(side, pair, bit, 1)
    side.finish()
    normed_0, cotangent = pair[0], pair[1]
    gate_0, up_0, down_0 = gate_job[2], up_job[2], down_job[2]

    gate_pre, up_value, hidden_0, part = first_forward(
        0, normed_0, gate_0, up_0, down_0, gate_step, up_step, down_step
    )

    side = Side()
    side.skip()
    gate_job1 = offsets_job(side, gate_codes, gate_zero, 1)
    up_job1 = offsets_job(side, up_codes, up_zero, 1)
    down_job1 = offsets_job(side, down_codes, down_zero, 1)
    grad_job = side.add(
        lambda c, s: hidden_grad_of(1, c, down_job1[2], s), cotangent, down_step
    )
    for bit in near:
        part = halve(side, part, bit)
    for bit in far:
        part = add_up(side, part, bit)
    state_1 = (state_0.astype(F32) + part).astype(BF16)
    normed_1 = norm_rows(state_1, norm_gain[1])
    for bit in reversed(near):
        normed_1 = double(side, normed_1, bit, 0)
    side.finish()
    gate_1, up_1, down_1, hidden_grad = gate_job1[2], up_job1[2], down_job1[2], grad_job[2]

    hidden_1, gate_grad, up_grad, part = last_layer(
        1, normed_1, hidden_grad, gate_1, up_1, gate_step, up_step
    )
    side = Side()
    side.skip()
    down_out = side.add(lambda x, u: step_grad(x, down_1, u, tiled, 1, None), hidden_1, cotangent)
    gate_out = side.add(lambda x, u: step_grad(x, gate_1, u, gate_step.shape, 1, None), normed_1, gate_grad)
    up_out = side.add(lambda x, u: step_grad(x, up_1, u, up_step.shape, 1, None), normed_1, up_grad)
    for bit in near:
        part = halve(side, part, bit)
    for bit in far:
        part = add_up(side, part, bit)
    cot_rows = (cot_rows.astype(F32) + norm_back(state_1, norm_gain[1], part)).astype(BF16)
    cotangent = cot_rows
    for bit in reversed(near):
        cotangent = double(side, cotangent, bit, 0)
    side.finish()
    down_out, gate_out, up_out = down_out[2], gate_out[2], up_out[2]

    gate_grad, up_grad, part = backward(
        0, cotangent, gate_pre, up_value, gate_0, up_0, down_0, gate_step, up_step, down_step
    )
    side = Side()
    side.skip()
    down_job = side.add(
        lambda x, u, e: step_grad(x, down_0, u, tiled, 0, e), hidden_0, cotangent, down_out
    )
    gate_job = side.add(
        lambda x, u, e: step_grad(x, gate_0, u, gate_step.shape, 0, e), normed_0, gate_grad, gate_out
    )
    up_job = side.add(lambda x, u, e: step_grad(x, up_0, u, up_step.shape, 0, e), normed_0, up_grad, up_out)
    for bit in near:
        part = halve(side, part, bit)
    for bit in far:
        part = halve(side, part, bit)
        half = cot_rows.shape[0] // 2
        cot_rows = lax.dynamic_slice_in_dim(cot_rows, own_bit(bit) * half, half, 0)
    side.finish()
    result = (cot_rows.astype(F32) + norm_back(tokens, norm_gain[0], part)).astype(BF16)
    return result, gate_job[2], up_job[2], down_job[2].reshape(down_shape)


def solution(mesh):
    placed = (
        P(("groups", "tensor"), None),
        P(),
        P(None, None, "tensor"),
        P(None, None, "tensor"),
        P(None, "tensor", None),
        P(None, None, "tensor"),
        P(None, None, "tensor"),
        P(None, "tensor", None),
        P(None, None, "tensor"),
        P(None, None, "tensor"),
        P(None, "tensor", None),
        P(("groups", "tensor"), None),
        P("groups", None),
    )
    return jax.shard_map(
        on_device,
        mesh=mesh,
        in_specs=placed,
        out_specs=(
            P(("groups", "tensor"), None),
            P("groups", None, "tensor"),
            P("groups", None, "tensor"),
            P("groups", "tensor", None),
        ),
        check_vma=False,
    )
```

```python
import functools

import jax
import jax.numpy as jnp
import numpy as np
from jax import lax
from jax.experimental import pallas as pl
from jax.experimental.pallas import tpu as pltpu
from jax.sharding import PartitionSpec as P

GROUP = 64
WORDS = GROUP // 4
LAYERS = 2
norm_epsilon = 1e-05
BF16 = jnp.bfloat16
F32 = jnp.float32
OFFSET = jnp.float8_e4m3fn
ANYWHERE = pl.BlockSpec(memory_space=pl.ANY)
IN_HBM = pl.BlockSpec(memory_space=pltpu.HBM)
SCALAR = pl.BlockSpec(memory_space=pltpu.SMEM)


def params(mib=60):
    return pltpu.CompilerParams(vmem_limit_bytes=mib * 2**20)


def cost(flops, bytes_accessed):
    return pl.CostEstimate(flops=int(flops), bytes_accessed=int(bytes_accessed), transcendentals=0)


def block_of(size, most):
    best = size
    if size > most:
        for candidate in range(128, most + 1, 128):
            if size % candidate == 0:
                best = candidate
    return best


def copy_in(source, target, sem):
    copy = pltpu.make_async_copy(source, target, sem)
    copy.start()
    return copy


def row_chunk(chunk, size):
    return pl.ds(pl.multiple_of(chunk * size, size), size)


def unpack(held, zeros, planes, slot):
    for piece in range(4):
        offset = ((held >> (2 * piece)) & 3) - zeros
        planes[slot, pl.ds(piece, WORDS, stride=4), :] = offset.astype(F32)


COUNT = 4
AHEAD = 2


def stream(count, copies, work, before=None, last=None, ahead=AHEAD):
    for chunk in range(min(ahead, count)):
        for copy in copies(chunk):
            copy.start()
    if before is not None:
        before()

    def step(chunk, _):
        for copy in copies(chunk):
            copy.wait()

        @pl.when(chunk + ahead < count)
        def _():
            for copy in copies(chunk + ahead):
                copy.start()

        if last is not None:
            @pl.when(chunk + ahead >= count)
            def _():
                last(chunk + ahead - count)

        work(chunk)
        return 0

    lax.fori_loop(0, count, step, 0)


def offsets_kernel(layer, half, *refs):
    code_any, zero_any = refs[:2]
    out_any, code, zero, out, planes, sems = refs[-6:]
    words, width = code.shape
    count = COUNT
    rows = words // count
    groups = rows // WORDS
    tile = planes.shape[-1]

    def code_copy(chunk):
        return pltpu.make_async_copy(
            code_any.at[layer, row_chunk(half * count + chunk, rows)],
            code.at[row_chunk(chunk, rows)],
            sems.at[chunk],
        )

    def out_copy(chunk):
        return pltpu.make_async_copy(
            out.at[row_chunk(chunk, rows * 4)],
            out_any.at[row_chunk(half * count + chunk, rows * 4)],
            sems.at[count + chunk],
        )

    own_groups = row_chunk(half, zero.shape[0])
    zero_copy = pltpu.make_async_copy(zero_any.at[layer, own_groups], zero, sems.at[2 * count])
    zero_copy.start()

    def work(chunk):
        def some_groups(block, _):
            first = chunk * groups + block * 8
            for index in range(width // tile):
                cols = slice(index * tile, (index + 1) * tile)
                zeros = zero[row_chunk(first // 8, 8), cols]
                for group in range(8):
                    held = code[row_chunk(first + group, WORDS), cols]
                    unpack(held, zeros[group : group + 1], planes, group)
                for group in range(8):
                    out[row_chunk(first + group, GROUP), cols] = planes[group].astype(OFFSET)
            return 0

        lax.fori_loop(0, groups // 8, some_groups, 0)
        out_copy(chunk).start()

    stream(count, lambda chunk: [code_copy(chunk)], work, zero_copy.wait)
    for chunk in range(count):
        out_copy(chunk).wait()


def offsets_of(codes, zeros, layer, earlier=None):
    _, words, width = codes.shape
    tile = 128 if width % 128 == 0 else 64
    operands = [codes, zeros] if earlier is None else [codes, zeros, earlier]
    return pl.pallas_call(
        functools.partial(offsets_kernel, layer, 0 if earlier is None else 1),
        in_specs=[IN_HBM] * len(operands),
        out_specs=IN_HBM,
        out_shape=jax.ShapeDtypeStruct((words * 4, width), OFFSET),
        scratch_shapes=[
            pltpu.VMEM((words // 2, width), jnp.int32),
            pltpu.VMEM((zeros.shape[1] // 2, width), jnp.int32),
            pltpu.VMEM((words * 2, width), OFFSET),
            pltpu.VMEM((8, GROUP, tile), F32),
            pltpu.SemaphoreType.DMA((2 * COUNT + 1,)),
        ],
        input_output_aliases={} if earlier is None else {2: 0},
        compiler_params=params(),
        cost_estimate=cost(words * width * 20, words * width * 4),
    )(*operands)


class DownCodes:
    def __init__(self, layer, code_any, zero_any, out_any, code, zero, out, planes, sems, half=0):
        self.half = half
        self.layer, self.code_any, self.zero_any, self.out_any = layer, code_any, zero_any, out_any
        self.code, self.zero, self.out, self.planes, self.sems = code, zero, out, planes, sems
        self.groups = code.shape[0] // WORDS
        self.lanes = code.shape[1] // COUNT
        self.tile = planes.shape[-1]
        self.tiles = self.lanes // self.tile

    def part(self, chunk):
        return (slice(None), row_chunk(chunk, self.lanes))

    def far_part(self, chunk):
        return self.part(self.half * COUNT + chunk)

    def zero_copy(self):
        own = row_chunk(self.half, self.zero.shape[-1])
        return pltpu.make_async_copy(
            self.zero_any.at[:, :, own], self.zero, self.sems.at[2 * COUNT]
        )

    def copy(self, chunk):
        return pltpu.make_async_copy(
            self.code_any.at[(self.layer,) + self.far_part(chunk)],
            self.code.at[self.part(chunk)],
            self.sems.at[chunk],
        )

    def out_copy(self, chunk):
        return pltpu.make_async_copy(
            self.out.at[self.part(chunk)],
            self.out_any.at[self.far_part(chunk)],
            self.sems.at[COUNT + chunk],
        )

    def tile_of(self, chunk, index):
        cols = pl.ds(pl.multiple_of(chunk * self.lanes + index * self.tile, self.tile), self.tile)
        for group in range(self.groups):
            held = self.code[group * WORDS : (group + 1) * WORDS, cols]
            zeros = self.zero[group, self.layer : self.layer + 1, cols]
            unpack(held, zeros, self.planes, group)
            self.out[group * GROUP : (group + 1) * GROUP, cols] = self.planes[group].astype(OFFSET)

    @staticmethod
    def scratch(codes, zeros, halves=1):
        _, words, width = codes.shape
        width = width // halves
        return [
            pltpu.VMEM((words, width), jnp.int32),
            pltpu.VMEM(zeros.shape[:2] + (width,), jnp.int32),
            pltpu.VMEM((words * 4, width), OFFSET),
            pltpu.VMEM((words // WORDS, GROUP, 128), F32),
            pltpu.SemaphoreType.DMA((2 * COUNT + 1,)),
        ]


def down_offsets_kernel(layer, half, *refs):
    code_any, zero_any = refs[:2]
    out_any, code, zero, out, planes, sems = refs[-6:]
    codes = DownCodes(layer, code_any, zero_any, out_any, code, zero, out, planes, sems, half)
    codes.zero_copy().start()

    def work(chunk):
        def tile(index, _):
            codes.tile_of(chunk, index)
            return 0

        lax.fori_loop(0, codes.tiles, tile, 0)
        codes.out_copy(chunk).start()

    stream(COUNT, lambda chunk: [codes.copy(chunk)], work, codes.zero_copy().wait)
    for chunk in range(COUNT):
        codes.out_copy(chunk).wait()


def down_offsets_of(codes, zeros, layer, earlier=None):
    _, words, width = codes.shape
    operands = [codes, zeros] if earlier is None else [codes, zeros, earlier]
    return pl.pallas_call(
        functools.partial(down_offsets_kernel, layer, 0 if earlier is None else 1),
        in_specs=[IN_HBM] * len(operands),
        out_specs=IN_HBM,
        out_shape=jax.ShapeDtypeStruct((words * 4, width), OFFSET),
        scratch_shapes=DownCodes.scratch(codes, zeros, 2),
        input_output_aliases={} if earlier is None else {2: 0},
        compiler_params=params(),
        cost_estimate=cost(words * width * 20, words * width * 4),
    )(*operands)


def sigmoid(value):
    return 1.0 / (1.0 + jnp.exp(-value))


def across(left, right):
    return lax.dot_general(left, right, (((1,), (1,)), ((), ())), preferred_element_type=F32)


def weights_of(offsets, steps):
    parts = []
    for group, step in enumerate(steps):
        part = offsets[group * GROUP : (group + 1) * GROUP].astype(F32)
        parts.append((part * step).astype(BF16))
    return jnp.concatenate(parts, axis=0)


def row_scale(value, step_most):
    top = jnp.max(jnp.abs(value), axis=1, keepdims=True) * step_most
    top = jnp.maximum(top, 1e-30)
    return 224.0 / top, top / 224.0


def across_offsets(scaled, offsets, steps):
    tokens = scaled.shape[0]
    found = []
    for first in range(0, len(steps), 4):
        count = min(4, len(steps) - first)
        high, low = [], []
        for step in steps[first : first + count]:
            part = scaled * step
            top = part.astype(OFFSET)
            high.append(top)
            low.append(((part - top.astype(F32)) * 16.0).astype(OFFSET))
        both = across(
            jnp.concatenate(high + low, axis=0),
            offsets[first * GROUP : (first + count) * GROUP, :],
        )
        rows = count * tokens
        both = both[:rows] + both[rows:] * (1.0 / 16.0)
        own = both[:tokens]
        lane_group = lax.broadcasted_iota(jnp.int32, own.shape, 1) // GROUP
        for group in range(1, count):
            own = jnp.where(lane_group == group, both[group * tokens : (group + 1) * tokens], own)
        found.append(own)
    return jnp.concatenate(found, axis=1)


class Matrix:
    def __init__(self, layer, source, step_source, offsets, steps, sems, by_rows):
        self.layer, self.source, self.step_source = layer, source, step_source
        self.offsets, self.steps, self.sems, self.by_rows = offsets, steps, sems, by_rows
        self.count = COUNT
        self.size = offsets.shape[0 if by_rows else 1] // self.count

    def part(self, chunk):
        if self.by_rows:
            return (row_chunk(chunk, self.size), slice(None))
        return (slice(None), row_chunk(chunk, self.size))

    def step_copy(self):
        source = self.step_source.at[self.layer] if self.by_rows else self.step_source
        return pltpu.make_async_copy(source, self.steps, self.sems.at[self.count])

    def copy(self, chunk):
        part = self.part(chunk)
        return pltpu.make_async_copy(self.source.at[part], self.offsets.at[part], self.sems.at[chunk])

    def weights(self, chunk):
        offsets = self.offsets[self.part(chunk)]
        groups = offsets.shape[0] // GROUP
        if self.by_rows:
            held = self.steps[row_chunk(chunk, groups), :]
            steps = [held[group : group + 1] for group in range(groups)]
        else:
            steps = self.step_rows(row_chunk(chunk, self.size))
        return weights_of(offsets, steps)

    def across(self, scaled, chunk):
        groups = self.size // GROUP
        held = self.steps[row_chunk(chunk, groups), :]
        steps = [held[group : group + 1] for group in range(groups)]
        return across_offsets(scaled, self.offsets[self.part(chunk)], steps)

    def step_rows(self, cols):
        layer = slice(self.layer, self.layer + 1)
        return [self.steps[group, layer, cols] for group in range(self.steps.shape[0])]

    def some_weights(self, chunk, piece, pieces):
        size = self.size // pieces
        if not self.by_rows:
            first = pl.multiple_of(chunk * self.size + piece * size, size)
            return weights_of(self.offsets[:, pl.ds(first, size)], self.step_rows(pl.ds(first, size)))
        groups = self.size // GROUP
        held = self.steps[row_chunk(chunk, groups), :]
        first = pl.multiple_of(chunk * self.size + piece * size, size)
        count = groups // pieces
        rows = range(piece * count, (piece + 1) * count)
        return weights_of(self.offsets[pl.ds(first, size), :], [held[row : row + 1] for row in rows])

    @staticmethod
    def scratch(offsets, steps):
        by_rows = offsets.shape[0] >= offsets.shape[1]
        return [
            pltpu.VMEM(offsets.shape, OFFSET),
            pltpu.VMEM(steps.shape[1:] if by_rows else steps.shape, F32),
            pltpu.SemaphoreType.DMA((COUNT + 1,)),
        ]


def gate_up_forward(x, gate, up, gate_out, up_out, before, beside=None, codes=None, after=None):
    pieces = 4

    def work(chunk):
        size = gate.size // pieces
        for piece in range(pieces):
            first = pl.multiple_of(chunk * gate.size + piece * size, size)
            rows = x[:, pl.ds(first, size)]
            for turn, (matrix, out) in enumerate(((gate, gate_out), (up, up_out))):
                weights = matrix.some_weights(chunk, piece, pieces)
                out[...] += jnp.dot(rows, weights, preferred_element_type=F32)
                if beside is not None:
                    beside(chunk, 2 * piece + turn, 2 * pieces)

    def ready():
        gate_out[...] = jnp.zeros_like(gate_out)
        up_out[...] = jnp.zeros_like(up_out)
        before()
        gate.step_copy().wait()
        up.step_copy().wait()

    gate.step_copy().start()
    up.step_copy().start()
    def copies(chunk):
        both = [gate.copy(chunk), up.copy(chunk)]
        return both if codes is None else both + [codes.copy(chunk)]

    def last(chunk):
        after.copy(chunk).start()

    stream(gate.count, copies, work, ready, None if after is None else last)
    gate_all = gate_out[...]
    return (gate_all * sigmoid(gate_all) * up_out[...]).astype(BF16)


def hidden_back(hidden_grad, gate_pre, up_value):
    gate_sigmoid = sigmoid(gate_pre)
    gate_grad = (
        hidden_grad * up_value * gate_sigmoid * (1.0 + gate_pre * (1.0 - gate_sigmoid))
    ).astype(BF16)
    up_grad = (hidden_grad * gate_pre * gate_sigmoid).astype(BF16)
    return gate_grad, up_grad


def gate_up_backward(gate_grad, up_grad, gate, up, scaled_gate, scaled_up):
    gate_value, up_value = gate_grad.astype(F32), up_grad.astype(F32)
    gate_factor, gate_back = row_scale(gate_value, jnp.max(gate.steps[...]))
    up_factor, up_back = row_scale(up_value, jnp.max(up.steps[...]))
    scaled_gate[...] = gate_value * gate_factor
    scaled_up[...] = up_value * up_factor

    def product(chunk):
        return (
            gate.across(scaled_gate[...], chunk) * gate_back
            + up.across(scaled_up[...], chunk) * up_back
        )

    return product


def cot_down(cot, down, out, pieces=4):
    most = jnp.max(down.steps[...])
    factor, back = row_scale(cot[...].astype(F32), most)
    size = down.size // pieces

    def work(chunk):
        for piece in range(pieces):
            cols = pl.ds(pl.multiple_of(chunk * down.size + piece * size, size), size)
            scaled = cot[:, cols].astype(F32) * factor
            out[...] += across_offsets(scaled, down.offsets[:, cols], down.step_rows(cols))

    return work, back


def halves_out(mine, part, kept_out, sent_out, cols):
    half = part.shape[0] // 2
    first, second = part[:half], part[half:]
    kept_out[:, cols] = jnp.where(mine == 0, first, second).astype(BF16)
    sent_out[:, cols] = jnp.where(mine == 0, second, first).astype(BF16)


def later(count, copies, work, last=None):
    def step(chunk, _):
        for copy in copies(chunk):
            copy.wait()

        @pl.when(chunk + AHEAD < count)
        def _():
            for copy in copies(chunk + AHEAD):
                copy.start()

        if last is not None:
            @pl.when(chunk + AHEAD >= count)
            def _():
                last(chunk + AHEAD - count)

        work(chunk)
        return 0

    lax.fori_loop(0, count, step, 0)


def first_forward_kernel(layer, mine, x_any, gate_any, up_any, code_any, zero_any, gs_any, us_any, ds_any, *refs):
    gate_out, up_out, hidden_out, kept_out, sent_out, off_any = refs[:6]
    x, sem = refs[6:8]
    gate = Matrix(layer, gate_any, gs_any, *refs[8:11], True)
    up = Matrix(layer, up_any, us_any, *refs[11:14], True)
    codes = DownCodes(layer, code_any, zero_any, off_any, *refs[14:19])
    down = Matrix(layer, off_any, ds_any, codes.out, *refs[19:21], False)
    x_copy = copy_in(x_any, x, sem.at[0])
    codes.zero_copy().start()
    down.step_copy().start()

    def before():
        x_copy.wait()
        codes.zero_copy().wait()

    def beside(chunk, turn, turns):
        for index in range(turn * codes.tiles // turns, (turn + 1) * codes.tiles // turns):
            codes.tile_of(chunk, index)

    hidden_out[...] = gate_up_forward(
        x, gate, up, gate_out, up_out, before, beside, codes
    )
    for chunk in range(COUNT):
        codes.out_copy(chunk).start()
    down.step_copy().wait()

    def work(chunk, _):
        part = jnp.dot(hidden_out[...], down.weights(chunk), preferred_element_type=F32)
        halves_out(mine[0], part, kept_out, sent_out, row_chunk(chunk, down.size))
        return 0

    lax.fori_loop(0, COUNT, work, 0)
    for chunk in range(COUNT):
        codes.out_copy(chunk).wait()


def first_forward(layer, mine, x, gate, up, down_codes, down_zero, gate_step, up_step, down_step):
    tokens, depth = x.shape
    width = gate.shape[1]
    return pl.pallas_call(
        functools.partial(first_forward_kernel, layer),
        in_specs=[SCALAR, ANYWHERE] + [IN_HBM] * 7,
        out_specs=[pl.BlockSpec(memory_space=pltpu.VMEM)] * 5 + [IN_HBM],
        out_shape=[
            jax.ShapeDtypeStruct((tokens, width), F32),
            jax.ShapeDtypeStruct((tokens, width), F32),
            jax.ShapeDtypeStruct((tokens, width), BF16),
            jax.ShapeDtypeStruct((tokens // 2, depth), BF16),
            jax.ShapeDtypeStruct((tokens // 2, depth), BF16),
            jax.ShapeDtypeStruct((width, depth), OFFSET),
        ],
        scratch_shapes=[pltpu.VMEM(x.shape, BF16), pltpu.SemaphoreType.DMA((1,))]
        + Matrix.scratch(gate, gate_step)
        + Matrix.scratch(up, up_step)
        + DownCodes.scratch(down_codes, down_zero)
        + [pltpu.VMEM(down_step.shape, F32), pltpu.SemaphoreType.DMA((COUNT + 1,))],
        compiler_params=params(),
        cost_estimate=cost(6 * tokens * depth * width, 4 * depth * width),
    )(mine, x, gate, up, down_codes, down_zero, gate_step, up_step, down_step)


def last_layer_kernel(layer, mine, x_any, cot_any, gate_any, up_any, down_any, gs_any, us_any, ds_any, *refs):
    hidden_out, gate_grad_out, up_grad_out, kept_out, sent_out = refs[:5]
    gate_pre, up_value, hidden_grad, scaled_gate, scaled_up, x, cot, sem = refs[5:13]
    gate = Matrix(layer, gate_any, gs_any, *refs[13:16], True)
    up = Matrix(layer, up_any, us_any, *refs[16:19], True)
    down = Matrix(layer, down_any, ds_any, *refs[19:22], False)
    x_copy = copy_in(x_any, x, sem.at[0])
    hidden_out[...] = gate_up_forward(x, gate, up, gate_pre, up_value, x_copy.wait, None, None, down)
    cot_copy = copy_in(cot_any, cot, sem.at[1])
    down.step_copy().start()
    cot_copy.wait()
    down.step_copy().wait()
    hidden_grad[...] = jnp.zeros_like(hidden_grad)
    down_work, back = cot_down(cot, down, hidden_grad)

    later(down.count, lambda chunk: [down.copy(chunk)], down_work)
    gate_grad, up_grad = hidden_back(hidden_grad[...] * back, gate_pre[...], up_value[...])
    gate_grad_out[...] = gate_grad
    up_grad_out[...] = up_grad
    product = gate_up_backward(gate_grad, up_grad, gate, up, scaled_gate, scaled_up)

    def work(chunk, _):
        halves_out(mine[0], product(chunk), kept_out, sent_out, row_chunk(chunk, gate.size))
        return 0

    lax.fori_loop(0, COUNT, work, 0)


def last_layer(layer, mine, x, cot, gate, up, down, gate_step, up_step, down_step):
    tokens, depth = x.shape
    width = gate.shape[1]
    small = jax.ShapeDtypeStruct((tokens, width), BF16)
    return pl.pallas_call(
        functools.partial(last_layer_kernel, layer),
        in_specs=[SCALAR] + [ANYWHERE] * 2 + [IN_HBM] * 6,
        out_shape=[
            small,
            small,
            small,
            jax.ShapeDtypeStruct((tokens // 2, depth), BF16),
            jax.ShapeDtypeStruct((tokens // 2, depth), BF16),
        ],
        scratch_shapes=[pltpu.VMEM((tokens, width), F32)] * 5
        + [
            pltpu.VMEM(x.shape, BF16),
            pltpu.VMEM(cot.shape, BF16),
            pltpu.SemaphoreType.DMA((2,)),
        ]
        + Matrix.scratch(gate, gate_step)
        + Matrix.scratch(up, up_step)
        + Matrix.scratch(down, down_step),
        compiler_params=params(),
        cost_estimate=cost(10 * tokens * depth * width, 4 * depth * width),
    )(mine, x, cot, gate, up, down, gate_step, up_step, down_step)


def backward_kernel(layer, mine, cot_any, pre_any, value_any, gate_any, up_any, down_any, gs_any, us_any, ds_any, *refs):
    gate_grad_out, up_grad_out, kept_out, sent_out = refs[:4]
    gate_pre, up_value, hidden_grad, scaled_gate, scaled_up, cot, sem = refs[4:11]
    gate = Matrix(layer, gate_any, gs_any, *refs[11:14], True)
    up = Matrix(layer, up_any, us_any, *refs[14:17], True)
    down = Matrix(layer, down_any, ds_any, *refs[17:20], False)
    cot_copy = copy_in(cot_any, cot, sem.at[0])
    down.step_copy().start()
    for chunk in range(AHEAD):
        down.copy(chunk).start()
    pre_copy = copy_in(pre_any, gate_pre, sem.at[1])
    value_copy = copy_in(value_any, up_value, sem.at[2])
    hidden_grad[...] = jnp.zeros_like(hidden_grad)
    cot_copy.wait()
    down.step_copy().wait()
    down_work, back = cot_down(cot, down, hidden_grad)

    def last(chunk):
        gate.copy(chunk).start()
        up.copy(chunk).start()

    later(down.count, lambda chunk: [down.copy(chunk)], down_work, last)
    gate.step_copy().start()
    up.step_copy().start()
    pre_copy.wait()
    value_copy.wait()
    gate_grad, up_grad = hidden_back(hidden_grad[...] * back, gate_pre[...], up_value[...])
    gate_grad_out[...] = gate_grad
    up_grad_out[...] = up_grad
    gate.step_copy().wait()
    up.step_copy().wait()
    product = gate_up_backward(gate_grad, up_grad, gate, up, scaled_gate, scaled_up)

    def work(chunk):
        halves_out(mine[0], product(chunk), kept_out, sent_out, row_chunk(chunk, gate.size))

    later(gate.count, lambda chunk: [gate.copy(chunk), up.copy(chunk)], work)


def backward(layer, mine, cot, gate_pre, up_value, gate, up, down, gate_step, up_step, down_step):
    tokens, depth = cot.shape
    width = gate.shape[1]
    small = jax.ShapeDtypeStruct((tokens, width), BF16)
    return pl.pallas_call(
        functools.partial(backward_kernel, layer),
        in_specs=[SCALAR] + [ANYWHERE] * 3 + [IN_HBM] * 6,
        out_shape=[small, small] + [jax.ShapeDtypeStruct((tokens // 2, depth), BF16)] * 2,
        scratch_shapes=[pltpu.VMEM((tokens, width), F32)] * 5
        + [pltpu.VMEM(cot.shape, BF16), pltpu.SemaphoreType.DMA((3,))]
        + Matrix.scratch(gate, gate_step)
        + Matrix.scratch(up, up_step)
        + Matrix.scratch(down, down_step),
        compiler_params=params(),
        cost_estimate=cost(6 * tokens * depth * width, 3 * depth * width),
    )(mine, cot, gate_pre, up_value, gate, up, down, gate_step, up_step, down_step)


def spread(x, groups):
    tokens = x.shape[0]
    tall = jnp.concatenate([x] * groups, axis=0)
    row_group = lax.broadcasted_iota(jnp.int32, tall.shape, 0) // tokens
    col_group = lax.broadcasted_iota(jnp.int32, tall.shape, 1) // GROUP
    return jnp.where(row_group == col_group, tall.astype(F32), 0.0).astype(BF16)


def step_grad_block(x, offsets, upstream):
    tokens = x.shape[0]
    rows = []
    groups = offsets.shape[0] // GROUP
    for first in range(0, groups, 4):
        count = min(4, groups - first)
        part = slice(first * GROUP, (first + count) * GROUP)
        product = jnp.dot(
            spread(x[:, part], count), offsets[part, :].astype(BF16), preferred_element_type=F32
        )
        for group in range(count):
            own = product[group * tokens : (group + 1) * tokens] * upstream
            rows.append(jnp.sum(own, axis=0, keepdims=True))
    return jnp.concatenate(rows, axis=0)


def step_grad_kernel(by_rows, half, halves, x_any, off_any, grad_any, *refs):
    out, x, offsets, grad, sem, sems = refs[-6:]
    count = COUNT // halves
    size = offsets.shape[0 if by_rows else 1] // count

    def places(chunk):
        chunk = row_chunk(chunk, size)
        return (chunk, slice(None)) if by_rows else (slice(None), chunk)

    def copy(chunk):
        return pltpu.make_async_copy(
            off_any.at[places(half * count + chunk)], offsets.at[places(chunk)], sems.at[chunk]
        )

    if by_rows:
        own = row_chunk(half, x.shape[1])
        x_copy = copy_in(x_any.at[:, own], x, sem.at[0])
        grad_copy = copy_in(grad_any, grad, sem.at[1])
    else:
        own = row_chunk(half, grad.shape[1])
        x_copy = copy_in(x_any, x, sem.at[0])
        grad_copy = copy_in(grad_any.at[:, own], grad, sem.at[1])
    def ready():
        x_copy.wait()
        grad_copy.wait()

    def work(chunk):
        part = row_chunk(chunk, size)
        if by_rows:
            out[row_chunk(chunk, size // GROUP), :] = step_grad_block(
                x[:, part], offsets[part, :], grad[...].astype(F32)
            )
        else:
            found = step_grad_block(x[...], offsets[:, part], grad[:, part].astype(F32))
            if len(out.shape) == 2:
                out[:, part] = found
            else:
                other = refs[0][:, part]
                for place in range(out.shape[0]):
                    out[place, 0:1, part] = found[place : place + 1]
                    out[place, 1:2, part] = other[place : place + 1]

    stream(count, lambda chunk: [copy(chunk)], work, ready)


def step_grad(x, offsets, upstream, layer, half, halves, earlier, last=None):
    tokens, depth = x.shape
    width = offsets.shape[1]
    groups = depth // GROUP
    by_rows = depth >= width
    operands = [x, offsets, upstream]
    in_specs = [ANYWHERE, IN_HBM, ANYWHERE]
    scratch = [x.shape, offsets.shape, upstream.shape]
    if by_rows:
        shape = (LAYERS, groups, width)
        out_spec = pl.BlockSpec((None, groups // halves, width), lambda i: (layer, half, 0))
        scratch[0] = (tokens, depth // halves)
        scratch[1] = (depth // halves, width)
    else:
        shape = (groups, width) if last is None else (groups, LAYERS, width)
        block = shape[:-1] + (width // halves,)
        out_spec = pl.BlockSpec(block, lambda i: (0,) * (len(shape) - 1) + (half,))
        scratch[1] = (depth, width // halves)
        scratch[2] = (tokens, width // halves)
    if last is not None:
        operands.append(last)
        in_specs.append(pl.BlockSpec((groups, width // halves), lambda i: (0, half)))
    aliases = {}
    if earlier is not None:
        aliases = {len(operands): 0}
        operands.append(earlier)
        in_specs.append(IN_HBM)
    return pl.pallas_call(
        functools.partial(step_grad_kernel, by_rows, half, halves),
        grid=(1,),
        in_specs=in_specs,
        out_specs=out_spec,
        out_shape=jax.ShapeDtypeStruct(shape, F32),
        scratch_shapes=[
            pltpu.VMEM(scratch[0], BF16),
            pltpu.VMEM(scratch[1], OFFSET),
            pltpu.VMEM(scratch[2], BF16),
            pltpu.SemaphoreType.DMA((2,)),
            pltpu.SemaphoreType.DMA((COUNT,)),
        ],
        input_output_aliases=aliases,
        compiler_params=params(),
        cost_estimate=cost(8 * tokens * depth * width // halves, depth * width // halves),
    )(*operands)


class Side:
    def __init__(self, *jobs):
        self.jobs = list(jobs)

    def swap(self, value, bit):
        count = lax.axis_size("tensor")
        pairs = [(i, i ^ bit) for i in range(count)]
        job = self.jobs.pop(0) if self.jobs else None
        if job is None:
            return lax.ppermute(value, "tensor", pairs)
        call, operands, results = job
        value, operands = lax.optimization_barrier((value, operands))
        got = lax.ppermute(value, "tensor", pairs)
        found = call(*operands, results.get("value"))
        got, results["value"] = lax.optimization_barrier((got, found))
        return got


def own_bit(bit):
    return (lax.axis_index("tensor") // bit) % 2


def halve_first(side, kept, sent, bit):
    return kept.astype(F32) + side.swap(sent, bit).astype(F32)


def halve(side, value, bit):
    half = value.shape[0] // 2
    mine = own_bit(bit)
    kept = lax.dynamic_slice_in_dim(value, mine * half, half, 0)
    sent = lax.dynamic_slice_in_dim(value, (1 - mine) * half, half, 0)
    got = side.swap(sent.astype(BF16), bit)
    return kept.astype(F32) + got.astype(F32)


def add_up(side, value, bit):
    rounded = value.astype(BF16)
    return rounded.astype(F32) + side.swap(rounded, bit).astype(F32)


def double(side, value, bit, axis):
    other = side.swap(value, bit)
    mine = own_bit(bit) == 0
    return jnp.concatenate(
        [jnp.where(mine, value, other), jnp.where(mine, other, value)], axis=axis
    )


def inverse_rms(values):
    return lax.rsqrt(jnp.mean(values * values, axis=-1, keepdims=True) + norm_epsilon)


def norm_rows(state, gain):
    values = state.astype(F32)
    return (values * inverse_rms(values) * gain).astype(BF16)


def norm_back(state, gain, upstream):
    values = state.astype(F32)
    scale = inverse_rms(values)
    normal = values * scale
    inner = upstream * gain
    return scale * (inner - normal * jnp.mean(inner * normal, axis=-1, keepdims=True))


def token_lengths(doc_lengths, index_rows, micro_rows):
    batch_index = index_rows // micro_rows
    position = index_rows % micro_rows
    picked = batch_index[:, None] == jnp.arange(doc_lengths.shape[0], dtype=jnp.int32)[None, :]
    chosen = jnp.sum(jnp.where(picked[:, :, None], doc_lengths[None, :, :], 0), axis=1)
    ends = jnp.sum(
        jnp.where(
            jnp.arange(chosen.shape[1])[:, None] <= jnp.arange(chosen.shape[1])[None, :],
            chosen[:, :, None],
            0,
        ),
        axis=1,
    )
    starts = ends - chosen
    inside = (position[:, None] >= starts) & (position[:, None] < ends)
    return jnp.sum(jnp.where(inside, chosen, 0), axis=1).astype(F32)


def on_device(
    tokens,
    norm_gain,
    gate_codes,
    up_codes,
    down_codes,
    gate_zero,
    up_zero,
    down_zero,
    gate_step,
    up_step,
    down_step,
    out_grad,
    doc_lengths,
):
    shard_rows, features = tokens.shape
    device_count = lax.axis_size("tensor")
    micro_rows = shard_rows * device_count // doc_lengths.shape[0]
    bits = [1 << k for k in range(device_count.bit_length() - 1)]
    near, far = bits[:-2], bits[-2:]

    far_count = 1 << len(far)
    far_index = np.arange(far_count)
    far_place = sum(((far_index >> k) & 1) << (len(far) - 1 - k) for k in range(len(far)))
    far_device = np.argsort(far_place)
    near_part = lax.axis_index("tensor") % (1 << len(near))
    device_ids = near_part + jnp.asarray(far_device << len(near), jnp.int32)
    row_ids = (
        device_ids[:, None] * shard_rows + jnp.arange(shard_rows, dtype=jnp.int32)[None, :]
    ).reshape(-1)
    lengths = token_lengths(doc_lengths, row_ids, micro_rows)

    down_step, down_zero = down_step.transpose(1, 0, 2), down_zero.transpose(1, 0, 2)

    def offsets_jobs(codes, zeros, layer, unpack_half=offsets_of):
        results = {}
        call = lambda c, z, earlier: unpack_half(c, z, layer, earlier)
        return [(call, (codes, zeros), results)] * 2, results

    gate_jobs, gate_0 = offsets_jobs(gate_codes, gate_zero, 0)
    up_jobs, up_0 = offsets_jobs(up_codes, up_zero, 0)
    side = Side(*gate_jobs, *up_jobs)
    pair = jnp.stack([tokens, out_grad])
    for bit in reversed(far):
        pair = double(side, pair, bit, 1)
    state_0 = pair[0]
    cot_rows = (pair[1].astype(F32) / lengths[:, None]).astype(BF16)
    pair = jnp.stack([norm_rows(pair[0], norm_gain[0]), cot_rows])
    for bit in reversed(near):
        pair = double(side, pair, bit, 1)
    normed_0, cotangent = pair[0], pair[1]
    gate_0, up_0 = gate_0["value"], up_0["value"]

    mine = own_bit(near[0]).reshape(1).astype(jnp.int32)
    gate_pre, up_value, hidden_0, kept, sent, down_0 = first_forward(
        0, mine, normed_0, gate_0, up_0, down_codes, down_zero, gate_step, up_step, down_step
    )

    gate_jobs, gate_1 = offsets_jobs(gate_codes, gate_zero, 1)
    up_jobs, up_1 = offsets_jobs(up_codes, up_zero, 1)
    down_jobs, down_1 = offsets_jobs(down_codes, down_zero, 1, down_offsets_of)
    side = Side(None, gate_jobs[0], *down_jobs, gate_jobs[1], *up_jobs)
    part = halve_first(side, kept, sent, near[0])
    for bit in near[1:]:
        part = halve(side, part, bit)
    for bit in far:
        part = add_up(side, part, bit)
    state_1 = (state_0.astype(F32) + part).astype(BF16)
    normed_1 = norm_rows(state_1, norm_gain[1])
    for bit in reversed(near):
        normed_1 = double(side, normed_1, bit, 0)
    gate_1, up_1, down_1 = gate_1["value"], up_1["value"], down_1["value"]

    hidden_1, gate_grad, up_grad, kept, sent = last_layer(
        1, mine, normed_1, cotangent, gate_1, up_1, down_1, gate_step, up_step, down_step
    )

    down_out, gate_out, up_out = {}, {}, {}

    def half_jobs(x, offsets, upstream, results):
        return [
            (
                lambda x, u, earlier, half=half: step_grad(x, offsets, u, 1, half, 2, earlier),
                (x, upstream),
                results,
            )
            for half in range(2)
        ]

    side = Side(
        None,
        *half_jobs(hidden_1, down_1, cotangent, down_out),
        *half_jobs(normed_1, gate_1, gate_grad, gate_out),
        *half_jobs(normed_1, up_1, up_grad, up_out),
    )
    part = halve_first(side, kept, sent, near[0])
    for bit in near[1:]:
        part = halve(side, part, bit)
    for bit in far:
        part = add_up(side, part, bit)
    cot_rows = (cot_rows.astype(F32) + norm_back(state_1, norm_gain[1], part)).astype(BF16)
    cotangent = cot_rows
    for bit in reversed(near):
        cotangent = double(side, cotangent, bit, 0)

    gate_grad, up_grad, kept, sent = backward(
        0,
        mine,
        cotangent,
        gate_pre,
        up_value,
        gate_0,
        up_0,
        down_0,
        gate_step,
        up_step,
        down_step,
    )
    last = down_out["value"]
    down_out = {}
    side = Side(
        None,
        (
            lambda x, u, earlier: step_grad(x, down_0, u, 0, 0, 1, earlier, last),
            (hidden_0, cotangent),
            down_out,
        ),
        (
            lambda x, u, earlier: step_grad(x, gate_0, u, 0, 0, 1, earlier),
            (normed_0, gate_grad),
            gate_out,
        ),
        (
            lambda x, u, earlier: step_grad(x, up_0, u, 0, 0, 1, earlier),
            (normed_0, up_grad),
            up_out,
        ),
    )
    part = halve_first(side, kept, sent, near[0])
    for bit in near[1:]:
        part = halve(side, part, bit)
    for bit in far:
        part = halve(side, part, bit)
        half = cot_rows.shape[0] // 2
        cot_rows = lax.dynamic_slice_in_dim(cot_rows, own_bit(bit) * half, half, 0)
    result = (cot_rows.astype(F32) + norm_back(tokens, norm_gain[0], part)).astype(BF16)
    return result, gate_out["value"], up_out["value"], down_out["value"].transpose(1, 0, 2)


def solution(mesh):
    placed = (
        P(("groups", "tensor"), None),
        P(),
        P(None, None, "tensor"),
        P(None, None, "tensor"),
        P(None, "tensor", None),
        P(None, None, "tensor"),
        P(None, None, "tensor"),
        P(None, "tensor", None),
        P(None, None, "tensor"),
        P(None, None, "tensor"),
        P(None, "tensor", None),
        P(("groups", "tensor"), None),
        P("groups", None),
    )
    return jax.shard_map(
        on_device,
        mesh=mesh,
        in_specs=placed,
        out_specs=(
            P(("groups", "tensor"), None),
            P("groups", None, "tensor"),
            P("groups", None, "tensor"),
            P("groups", "tensor", None),
        ),
        check_vma=False,
    )
```

```python
import functools

import jax
import jax.numpy as jnp
import numpy as np
from jax import lax
from jax.experimental import pallas as pl
from jax.experimental.pallas import tpu as pltpu
from jax.sharding import PartitionSpec as P

GROUP = 64
WORDS = GROUP // 4
LAYERS = 2
norm_epsilon = 1e-05
BF16 = jnp.bfloat16
F32 = jnp.float32
OFFSET = jnp.float8_e4m3fn
ANYWHERE = pl.BlockSpec(memory_space=pl.ANY)
IN_HBM = pl.BlockSpec(memory_space=pltpu.HBM)
SCALAR = pl.BlockSpec(memory_space=pltpu.SMEM)


def params(mib=60):
    return pltpu.CompilerParams(vmem_limit_bytes=mib * 2**20)


def cost(flops, bytes_accessed):
    return pl.CostEstimate(flops=int(flops), bytes_accessed=int(bytes_accessed), transcendentals=0)


def block_of(size, most):
    best = size
    if size > most:
        for candidate in range(128, most + 1, 128):
            if size % candidate == 0:
                best = candidate
    return best


def copy_in(source, target, sem):
    copy = pltpu.make_async_copy(source, target, sem)
    copy.start()
    return copy


def row_chunk(chunk, size):
    return pl.ds(pl.multiple_of(chunk * size, size), size)


def unpack(held, zeros, planes, slot):
    for piece in range(4):
        offset = ((held >> (2 * piece)) & 3) - zeros
        planes[slot, pl.ds(piece, WORDS, stride=4), :] = offset.astype(F32)


COUNT = 4
AHEAD = 2


def stream(count, copies, work, before=None, last=None, ahead=AHEAD):
    for chunk in range(min(ahead, count)):
        for copy in copies(chunk):
            copy.start()
    if before is not None:
        before()

    def step(chunk, _):
        for copy in copies(chunk):
            copy.wait()

        @pl.when(chunk + ahead < count)
        def _():
            for copy in copies(chunk + ahead):
                copy.start()

        if last is not None:
            @pl.when(chunk + ahead >= count)
            def _():
                last(chunk + ahead - count)

        work(chunk)
        return 0

    lax.fori_loop(0, count, step, 0)


def offsets_kernel(layer, half, halves, *refs):
    code_any, zero_any = refs[:2]
    out_any, code, zero, out, planes, sems = refs[-6:]
    words, width = code.shape
    count = 2 * COUNT // halves
    rows = words // count
    groups = rows // WORDS
    tile = planes.shape[-1]

    def code_copy(chunk):
        return pltpu.make_async_copy(
            code_any.at[layer, row_chunk(half * count + chunk, rows)],
            code.at[row_chunk(chunk, rows)],
            sems.at[chunk],
        )

    def out_copy(chunk):
        return pltpu.make_async_copy(
            out.at[row_chunk(chunk, rows * 4)],
            out_any.at[row_chunk(half * count + chunk, rows * 4)],
            sems.at[count + chunk],
        )

    own_groups = row_chunk(half, zero.shape[0])
    zero_copy = pltpu.make_async_copy(zero_any.at[layer, own_groups], zero, sems.at[2 * count])
    zero_copy.start()

    def work(chunk):
        def some_groups(block, _):
            first = chunk * groups + block * 8
            for index in range(width // tile):
                cols = slice(index * tile, (index + 1) * tile)
                zeros = zero[row_chunk(first // 8, 8), cols]
                for group in range(8):
                    held = code[row_chunk(first + group, WORDS), cols]
                    unpack(held, zeros[group : group + 1], planes, group)
                for group in range(8):
                    out[row_chunk(first + group, GROUP), cols] = planes[group].astype(OFFSET)
            return 0

        lax.fori_loop(0, groups // 8, some_groups, 0)
        out_copy(chunk).start()

    stream(count, lambda chunk: [code_copy(chunk)], work, zero_copy.wait)
    for chunk in range(count):
        out_copy(chunk).wait()


def offsets_of(codes, zeros, layer, earlier=None, halves=2):
    _, words, width = codes.shape
    tile = 128 if width % 128 == 0 else 64
    operands = [codes, zeros] if earlier is None else [codes, zeros, earlier]
    return pl.pallas_call(
        functools.partial(offsets_kernel, layer, 0 if earlier is None else 1, halves),
        in_specs=[IN_HBM] * len(operands),
        out_specs=IN_HBM,
        out_shape=jax.ShapeDtypeStruct((words * 4, width), OFFSET),
        scratch_shapes=[
            pltpu.VMEM((words // halves, width), jnp.int32),
            pltpu.VMEM((zeros.shape[1] // halves, width), jnp.int32),
            pltpu.VMEM((words * 4 // halves, width), OFFSET),
            pltpu.VMEM((8, GROUP, tile), F32),
            pltpu.SemaphoreType.DMA((4 * COUNT // halves + 1,)),
        ],
        input_output_aliases={} if earlier is None else {2: 0},
        compiler_params=params(),
        cost_estimate=cost(words * width * 40 // halves, words * width * 8 // halves),
    )(*operands)


class DownCodes:
    def __init__(self, layer, code_any, zero_any, out_any, code, zero, out, planes, sems, half=0):
        self.half = half
        self.layer, self.code_any, self.zero_any, self.out_any = layer, code_any, zero_any, out_any
        self.code, self.zero, self.out, self.planes, self.sems = code, zero, out, planes, sems
        self.groups = code.shape[0] // WORDS
        self.lanes = code.shape[1] // COUNT
        self.tile = planes.shape[-1]
        self.tiles = self.lanes // self.tile

    def part(self, chunk):
        return (slice(None), row_chunk(chunk, self.lanes))

    def far_part(self, chunk):
        return self.part(self.half * COUNT + chunk)

    def zero_copy(self):
        own = row_chunk(self.half, self.zero.shape[-1])
        return pltpu.make_async_copy(
            self.zero_any.at[:, :, own], self.zero, self.sems.at[2 * COUNT]
        )

    def copy(self, chunk):
        return pltpu.make_async_copy(
            self.code_any.at[(self.layer,) + self.far_part(chunk)],
            self.code.at[self.part(chunk)],
            self.sems.at[chunk],
        )

    def out_copy(self, chunk):
        return pltpu.make_async_copy(
            self.out.at[self.part(chunk)],
            self.out_any.at[self.far_part(chunk)],
            self.sems.at[COUNT + chunk],
        )

    def tile_of(self, chunk, index):
        cols = pl.ds(pl.multiple_of(chunk * self.lanes + index * self.tile, self.tile), self.tile)
        for group in range(self.groups):
            held = self.code[group * WORDS : (group + 1) * WORDS, cols]
            zeros = self.zero[group, self.layer : self.layer + 1, cols]
            unpack(held, zeros, self.planes, group)
            self.out[group * GROUP : (group + 1) * GROUP, cols] = self.planes[group].astype(OFFSET)

    @staticmethod
    def scratch(codes, zeros, halves=1):
        _, words, width = codes.shape
        width = width // halves
        return [
            pltpu.VMEM((words, width), jnp.int32),
            pltpu.VMEM(zeros.shape[:2] + (width,), jnp.int32),
            pltpu.VMEM((words * 4, width), OFFSET),
            pltpu.VMEM((words // WORDS, GROUP, 128), F32),
            pltpu.SemaphoreType.DMA((2 * COUNT + 1,)),
        ]


def down_offsets_kernel(layer, half, *refs):
    code_any, zero_any = refs[:2]
    out_any, code, zero, out, planes, sems = refs[-6:]
    codes = DownCodes(layer, code_any, zero_any, out_any, code, zero, out, planes, sems, half)
    codes.zero_copy().start()

    def work(chunk):
        def tile(index, _):
            codes.tile_of(chunk, index)
            return 0

        lax.fori_loop(0, codes.tiles, tile, 0)
        codes.out_copy(chunk).start()

    stream(COUNT, lambda chunk: [codes.copy(chunk)], work, codes.zero_copy().wait)
    for chunk in range(COUNT):
        codes.out_copy(chunk).wait()


def down_offsets_of(codes, zeros, layer, earlier=None):
    _, words, width = codes.shape
    operands = [codes, zeros] if earlier is None else [codes, zeros, earlier]
    return pl.pallas_call(
        functools.partial(down_offsets_kernel, layer, 0 if earlier is None else 1),
        in_specs=[IN_HBM] * len(operands),
        out_specs=IN_HBM,
        out_shape=jax.ShapeDtypeStruct((words * 4, width), OFFSET),
        scratch_shapes=DownCodes.scratch(codes, zeros, 2),
        input_output_aliases={} if earlier is None else {2: 0},
        compiler_params=params(),
        cost_estimate=cost(words * width * 20, words * width * 4),
    )(*operands)


def sigmoid(value):
    return 1.0 / (1.0 + jnp.exp(-value))


def across(left, right):
    return lax.dot_general(left, right, (((1,), (1,)), ((), ())), preferred_element_type=F32)


def weights_of(offsets, steps):
    parts = []
    for group, step in enumerate(steps):
        part = offsets[group * GROUP : (group + 1) * GROUP].astype(BF16)
        parts.append(part * jnp.broadcast_to(step, part.shape).astype(BF16))
    return jnp.concatenate(parts, axis=0)


def row_scale(value, step_most):
    top = jnp.max(jnp.abs(value), axis=1, keepdims=True) * step_most
    top = jnp.maximum(top, 1e-30)
    return 224.0 / top, top / 224.0


def across_offsets(scaled, offsets, steps):
    tokens = scaled.shape[0]
    found = []
    for first in range(0, len(steps), 4):
        count = min(4, len(steps) - first)
        high, low = [], []
        for step in steps[first : first + count]:
            part = scaled * step
            top = part.astype(OFFSET)
            high.append(top)
            low.append(((part - top.astype(F32)) * 16.0).astype(OFFSET))
        both = across(
            jnp.concatenate(high + low, axis=0),
            offsets[first * GROUP : (first + count) * GROUP, :],
        )
        rows = count * tokens
        both = both[:rows] + both[rows:] * (1.0 / 16.0)
        own = both[:tokens]
        lane_group = lax.broadcasted_iota(jnp.int32, own.shape, 1) // GROUP
        for group in range(1, count):
            own = jnp.where(lane_group == group, both[group * tokens : (group + 1) * tokens], own)
        found.append(own)
    return jnp.concatenate(found, axis=1)


class Matrix:
    def __init__(self, layer, source, step_source, offsets, steps, sems, by_rows):
        self.layer, self.source, self.step_source = layer, source, step_source
        self.offsets, self.steps, self.sems, self.by_rows = offsets, steps, sems, by_rows
        self.count = COUNT
        self.size = offsets.shape[0 if by_rows else 1] // self.count

    def part(self, chunk):
        if self.by_rows:
            return (row_chunk(chunk, self.size), slice(None))
        return (slice(None), row_chunk(chunk, self.size))

    def step_copy(self):
        source = self.step_source.at[self.layer] if self.by_rows else self.step_source
        return pltpu.make_async_copy(source, self.steps, self.sems.at[self.count])

    def copy(self, chunk):
        part = self.part(chunk)
        return pltpu.make_async_copy(self.source.at[part], self.offsets.at[part], self.sems.at[chunk])

    def weights(self, chunk):
        offsets = self.offsets[self.part(chunk)]
        groups = offsets.shape[0] // GROUP
        if self.by_rows:
            held = self.steps[row_chunk(chunk, groups), :]
            steps = [held[group : group + 1] for group in range(groups)]
        else:
            steps = self.step_rows(row_chunk(chunk, self.size))
        return weights_of(offsets, steps)

    def across(self, scaled, chunk):
        groups = self.size // GROUP
        held = self.steps[row_chunk(chunk, groups), :]
        steps = [held[group : group + 1] for group in range(groups)]
        return across_offsets(scaled, self.offsets[self.part(chunk)], steps)

    def step_rows(self, cols):
        layer = slice(self.layer, self.layer + 1)
        return [self.steps[group, layer, cols] for group in range(self.steps.shape[0])]

    def some_weights(self, chunk, piece, pieces):
        size = self.size // pieces
        if not self.by_rows:
            first = pl.multiple_of(chunk * self.size + piece * size, size)
            return weights_of(self.offsets[:, pl.ds(first, size)], self.step_rows(pl.ds(first, size)))
        groups = self.size // GROUP
        held = self.steps[row_chunk(chunk, groups), :]
        first = pl.multiple_of(chunk * self.size + piece * size, size)
        count = groups // pieces
        rows = range(piece * count, (piece + 1) * count)
        return weights_of(self.offsets[pl.ds(first, size), :], [held[row : row + 1] for row in rows])

    @staticmethod
    def scratch(offsets, steps):
        by_rows = offsets.shape[0] >= offsets.shape[1]
        return [
            pltpu.VMEM(offsets.shape, OFFSET),
            pltpu.VMEM(steps.shape[1:] if by_rows else steps.shape, F32),
            pltpu.SemaphoreType.DMA((COUNT + 1,)),
        ]


def gate_up_forward(x, gate, up, gate_out, up_out, before, beside=None, codes=None, after=None):
    pieces = 4

    def work(chunk):
        size = gate.size // pieces
        for piece in range(pieces):
            first = pl.multiple_of(chunk * gate.size + piece * size, size)
            rows = x[:, pl.ds(first, size)]
            for turn, (matrix, out) in enumerate(((gate, gate_out), (up, up_out))):
                weights = matrix.some_weights(chunk, piece, pieces)
                out[...] += jnp.dot(rows, weights, preferred_element_type=F32)
                if beside is not None:
                    beside(chunk, 2 * piece + turn, 2 * pieces)

    def ready():
        gate_out[...] = jnp.zeros_like(gate_out)
        up_out[...] = jnp.zeros_like(up_out)
        before()
        gate.step_copy().wait()
        up.step_copy().wait()

    gate.step_copy().start()
    up.step_copy().start()
    def copies(chunk):
        both = [gate.copy(chunk), up.copy(chunk)]
        return both if codes is None else both + [codes.copy(chunk)]

    def last(chunk):
        after.copy(chunk).start()

    stream(gate.count, copies, work, ready, None if after is None else last)
    gate_all = gate_out[...]
    return (gate_all * sigmoid(gate_all) * up_out[...]).astype(BF16)


def hidden_back(hidden_grad, gate_pre, up_value):
    gate_sigmoid = sigmoid(gate_pre)
    gate_grad = (
        hidden_grad * up_value * gate_sigmoid * (1.0 + gate_pre * (1.0 - gate_sigmoid))
    ).astype(BF16)
    up_grad = (hidden_grad * gate_pre * gate_sigmoid).astype(BF16)
    return gate_grad, up_grad


def gate_up_backward(gate_grad, up_grad, gate, up, scaled_gate, scaled_up):
    gate_value, up_value = gate_grad.astype(F32), up_grad.astype(F32)
    gate_factor, gate_back = row_scale(gate_value, jnp.max(gate.steps[...]))
    up_factor, up_back = row_scale(up_value, jnp.max(up.steps[...]))
    scaled_gate[...] = gate_value * gate_factor
    scaled_up[...] = up_value * up_factor

    def product(chunk):
        return (
            gate.across(scaled_gate[...], chunk) * gate_back
            + up.across(scaled_up[...], chunk) * up_back
        )

    return product


def cot_down(cot, down, out, pieces=4):
    most = jnp.max(down.steps[...])
    factor, back = row_scale(cot[...].astype(F32), most)
    size = down.size // pieces

    def work(chunk):
        for piece in range(pieces):
            cols = pl.ds(pl.multiple_of(chunk * down.size + piece * size, size), size)
            scaled = cot[:, cols].astype(F32) * factor
            out[...] += across_offsets(scaled, down.offsets[:, cols], down.step_rows(cols))

    return work, back


def halves_out(mine, part, kept_out, sent_out, cols):
    half = part.shape[0] // 2
    first, second = part[:half], part[half:]
    kept_out[:, cols] = jnp.where(mine == 0, first, second).astype(BF16)
    sent_out[:, cols] = jnp.where(mine == 0, second, first).astype(BF16)


def later(count, copies, work, last=None):
    def step(chunk, _):
        for copy in copies(chunk):
            copy.wait()

        @pl.when(chunk + AHEAD < count)
        def _():
            for copy in copies(chunk + AHEAD):
                copy.start()

        if last is not None:
            @pl.when(chunk + AHEAD >= count)
            def _():
                last(chunk + AHEAD - count)

        work(chunk)
        return 0

    lax.fori_loop(0, count, step, 0)


def first_forward_kernel(layer, mine, x_any, gate_any, up_any, code_any, zero_any, gs_any, us_any, ds_any, *refs):
    gate_out, up_out, hidden_out, kept_out, sent_out, off_any = refs[:6]
    x, sem = refs[6:8]
    gate = Matrix(layer, gate_any, gs_any, *refs[8:11], True)
    up = Matrix(layer, up_any, us_any, *refs[11:14], True)
    codes = DownCodes(layer, code_any, zero_any, off_any, *refs[14:19])
    down = Matrix(layer, off_any, ds_any, codes.out, *refs[19:21], False)
    x_copy = copy_in(x_any, x, sem.at[0])
    codes.zero_copy().start()
    down.step_copy().start()

    def before():
        x_copy.wait()
        codes.zero_copy().wait()

    def beside(chunk, turn, turns):
        for index in range(turn * codes.tiles // turns, (turn + 1) * codes.tiles // turns):
            codes.tile_of(chunk, index)

    hidden_out[...] = gate_up_forward(
        x, gate, up, gate_out, up_out, before, beside, codes
    )
    for chunk in range(COUNT):
        codes.out_copy(chunk).start()
    down.step_copy().wait()

    def work(chunk, _):
        part = jnp.dot(hidden_out[...], down.weights(chunk), preferred_element_type=F32)
        halves_out(mine[0], part, kept_out, sent_out, row_chunk(chunk, down.size))
        return 0

    lax.fori_loop(0, COUNT, work, 0)
    for chunk in range(COUNT):
        codes.out_copy(chunk).wait()


def first_forward(layer, mine, x, gate, up, down_codes, down_zero, gate_step, up_step, down_step):
    tokens, depth = x.shape
    width = gate.shape[1]
    return pl.pallas_call(
        functools.partial(first_forward_kernel, layer),
        in_specs=[SCALAR, ANYWHERE] + [IN_HBM] * 7,
        out_specs=[pl.BlockSpec(memory_space=pltpu.VMEM)] * 5 + [IN_HBM],
        out_shape=[
            jax.ShapeDtypeStruct((tokens, width), F32),
            jax.ShapeDtypeStruct((tokens, width), F32),
            jax.ShapeDtypeStruct((tokens, width), BF16),
            jax.ShapeDtypeStruct((tokens // 2, depth), BF16),
            jax.ShapeDtypeStruct((tokens // 2, depth), BF16),
            jax.ShapeDtypeStruct((width, depth), OFFSET),
        ],
        scratch_shapes=[pltpu.VMEM(x.shape, BF16), pltpu.SemaphoreType.DMA((1,))]
        + Matrix.scratch(gate, gate_step)
        + Matrix.scratch(up, up_step)
        + DownCodes.scratch(down_codes, down_zero)
        + [pltpu.VMEM(down_step.shape, F32), pltpu.SemaphoreType.DMA((COUNT + 1,))],
        compiler_params=params(),
        cost_estimate=cost(6 * tokens * depth * width, 4 * depth * width),
    )(mine, x, gate, up, down_codes, down_zero, gate_step, up_step, down_step)


def last_layer_kernel(layer, mine, x_any, cot_any, gate_any, up_any, down_any, gs_any, us_any, ds_any, *refs):
    hidden_out, gate_grad_out, up_grad_out, kept_out, sent_out = refs[:5]
    gate_pre, up_value, hidden_grad, scaled_gate, scaled_up, x, cot, sem = refs[5:13]
    gate = Matrix(layer, gate_any, gs_any, *refs[13:16], True)
    up = Matrix(layer, up_any, us_any, *refs[16:19], True)
    down = Matrix(layer, down_any, ds_any, *refs[19:22], False)
    x_copy = copy_in(x_any, x, sem.at[0])
    hidden_out[...] = gate_up_forward(x, gate, up, gate_pre, up_value, x_copy.wait, None, None, down)
    cot_copy = copy_in(cot_any, cot, sem.at[1])
    down.step_copy().start()
    cot_copy.wait()
    down.step_copy().wait()
    hidden_grad[...] = jnp.zeros_like(hidden_grad)
    down_work, back = cot_down(cot, down, hidden_grad)

    later(down.count, lambda chunk: [down.copy(chunk)], down_work)
    gate_grad, up_grad = hidden_back(hidden_grad[...] * back, gate_pre[...], up_value[...])
    gate_grad_out[...] = gate_grad
    up_grad_out[...] = up_grad
    product = gate_up_backward(gate_grad, up_grad, gate, up, scaled_gate, scaled_up)

    def work(chunk, _):
        halves_out(mine[0], product(chunk), kept_out, sent_out, row_chunk(chunk, gate.size))
        return 0

    lax.fori_loop(0, COUNT, work, 0)


def last_layer(layer, mine, x, cot, gate, up, down, gate_step, up_step, down_step):
    tokens, depth = x.shape
    width = gate.shape[1]
    small = jax.ShapeDtypeStruct((tokens, width), BF16)
    return pl.pallas_call(
        functools.partial(last_layer_kernel, layer),
        in_specs=[SCALAR] + [ANYWHERE] * 2 + [IN_HBM] * 6,
        out_shape=[
            small,
            small,
            small,
            jax.ShapeDtypeStruct((tokens // 2, depth), BF16),
            jax.ShapeDtypeStruct((tokens // 2, depth), BF16),
        ],
        scratch_shapes=[pltpu.VMEM((tokens, width), F32)] * 5
        + [
            pltpu.VMEM(x.shape, BF16),
            pltpu.VMEM(cot.shape, BF16),
            pltpu.SemaphoreType.DMA((2,)),
        ]
        + Matrix.scratch(gate, gate_step)
        + Matrix.scratch(up, up_step)
        + Matrix.scratch(down, down_step),
        compiler_params=params(),
        cost_estimate=cost(10 * tokens * depth * width, 4 * depth * width),
    )(mine, x, cot, gate, up, down, gate_step, up_step, down_step)


def backward_kernel(layer, mine, cot_any, pre_any, value_any, gate_any, up_any, down_any, gs_any, us_any, ds_any, *refs):
    gate_grad_out, up_grad_out, kept_out, sent_out = refs[:4]
    gate_pre, up_value, hidden_grad, scaled_gate, scaled_up, cot, sem = refs[4:11]
    gate = Matrix(layer, gate_any, gs_any, *refs[11:14], True)
    up = Matrix(layer, up_any, us_any, *refs[14:17], True)
    down = Matrix(layer, down_any, ds_any, *refs[17:20], False)
    cot_copy = copy_in(cot_any, cot, sem.at[0])
    down.step_copy().start()
    for chunk in range(AHEAD):
        down.copy(chunk).start()
    pre_copy = copy_in(pre_any, gate_pre, sem.at[1])
    value_copy = copy_in(value_any, up_value, sem.at[2])
    hidden_grad[...] = jnp.zeros_like(hidden_grad)
    cot_copy.wait()
    down.step_copy().wait()
    down_work, back = cot_down(cot, down, hidden_grad)

    def last(chunk):
        gate.copy(chunk).start()
        up.copy(chunk).start()

    later(down.count, lambda chunk: [down.copy(chunk)], down_work, last)
    gate.step_copy().start()
    up.step_copy().start()
    pre_copy.wait()
    value_copy.wait()
    gate_grad, up_grad = hidden_back(hidden_grad[...] * back, gate_pre[...], up_value[...])
    gate_grad_out[...] = gate_grad
    up_grad_out[...] = up_grad
    gate.step_copy().wait()
    up.step_copy().wait()
    product = gate_up_backward(gate_grad, up_grad, gate, up, scaled_gate, scaled_up)

    def work(chunk):
        halves_out(mine[0], product(chunk), kept_out, sent_out, row_chunk(chunk, gate.size))

    later(gate.count, lambda chunk: [gate.copy(chunk), up.copy(chunk)], work)


def backward(layer, mine, cot, gate_pre, up_value, gate, up, down, gate_step, up_step, down_step):
    tokens, depth = cot.shape
    width = gate.shape[1]
    small = jax.ShapeDtypeStruct((tokens, width), BF16)
    return pl.pallas_call(
        functools.partial(backward_kernel, layer),
        in_specs=[SCALAR] + [ANYWHERE] * 3 + [IN_HBM] * 6,
        out_shape=[small, small] + [jax.ShapeDtypeStruct((tokens // 2, depth), BF16)] * 2,
        scratch_shapes=[pltpu.VMEM((tokens, width), F32)] * 5
        + [pltpu.VMEM(cot.shape, BF16), pltpu.SemaphoreType.DMA((3,))]
        + Matrix.scratch(gate, gate_step)
        + Matrix.scratch(up, up_step)
        + Matrix.scratch(down, down_step),
        compiler_params=params(),
        cost_estimate=cost(6 * tokens * depth * width, 3 * depth * width),
    )(mine, cot, gate_pre, up_value, gate, up, down, gate_step, up_step, down_step)


def spread(x, groups):
    tokens = x.shape[0]
    tall = jnp.concatenate([x] * groups, axis=0)
    row_group = lax.broadcasted_iota(jnp.int32, tall.shape, 0) // tokens
    col_group = lax.broadcasted_iota(jnp.int32, tall.shape, 1) // GROUP
    return jnp.where(row_group == col_group, tall.astype(F32), 0.0).astype(BF16)


def step_grad_block(x, offsets, upstream):
    tokens = x.shape[0]
    rows = []
    groups = offsets.shape[0] // GROUP
    for first in range(0, groups, 4):
        count = min(4, groups - first)
        part = slice(first * GROUP, (first + count) * GROUP)
        product = jnp.dot(
            spread(x[:, part], count), offsets[part, :].astype(BF16), preferred_element_type=F32
        )
        for group in range(count):
            own = product[group * tokens : (group + 1) * tokens] * upstream
            rows.append(jnp.sum(own, axis=0, keepdims=True))
    return jnp.concatenate(rows, axis=0)


def step_grad_kernel(by_rows, half, halves, x_any, off_any, grad_any, *refs):
    out, x, offsets, grad, sem, sems = refs[-6:]
    count = COUNT // halves
    size = offsets.shape[0 if by_rows else 1] // count

    def places(chunk):
        chunk = row_chunk(chunk, size)
        return (chunk, slice(None)) if by_rows else (slice(None), chunk)

    def copy(chunk):
        return pltpu.make_async_copy(
            off_any.at[places(half * count + chunk)], offsets.at[places(chunk)], sems.at[chunk]
        )

    if by_rows:
        own = row_chunk(half, x.shape[1])
        x_copy = copy_in(x_any.at[:, own], x, sem.at[0])
        grad_copy = copy_in(grad_any, grad, sem.at[1])
    else:
        own = row_chunk(half, grad.shape[1])
        x_copy = copy_in(x_any, x, sem.at[0])
        grad_copy = copy_in(grad_any.at[:, own], grad, sem.at[1])
    def ready():
        x_copy.wait()
        grad_copy.wait()

    def work(chunk):
        part = row_chunk(chunk, size)
        if by_rows:
            out[row_chunk(chunk, size // GROUP), :] = step_grad_block(
                x[:, part], offsets[part, :], grad[...].astype(F32)
            )
        else:
            found = step_grad_block(x[...], offsets[:, part], grad[:, part].astype(F32))
            if len(out.shape) == 2:
                out[:, part] = found
            else:
                other = refs[0][:, part]
                for place in range(out.shape[0]):
                    out[place, 0:1, part] = found[place : place + 1]
                    out[place, 1:2, part] = other[place : place + 1]

    stream(count, lambda chunk: [copy(chunk)], work, ready)


def step_grad(x, offsets, upstream, layer, half, halves, earlier, last=None):
    tokens, depth = x.shape
    width = offsets.shape[1]
    groups = depth // GROUP
    by_rows = depth >= width
    operands = [x, offsets, upstream]
    in_specs = [ANYWHERE, IN_HBM, ANYWHERE]
    scratch = [x.shape, offsets.shape, upstream.shape]
    if by_rows:
        shape = (LAYERS, groups, width)
        out_spec = pl.BlockSpec((None, groups // halves, width), lambda i: (layer, half, 0))
        scratch[0] = (tokens, depth // halves)
        scratch[1] = (depth // halves, width)
    else:
        shape = (groups, width) if last is None else (groups, LAYERS, width)
        block = shape[:-1] + (width // halves,)
        out_spec = pl.BlockSpec(block, lambda i: (0,) * (len(shape) - 1) + (half,))
        scratch[1] = (depth, width // halves)
        scratch[2] = (tokens, width // halves)
    if last is not None:
        operands.append(last)
        in_specs.append(pl.BlockSpec((groups, width // halves), lambda i: (0, half)))
    aliases = {}
    if earlier is not None:
        aliases = {len(operands): 0}
        operands.append(earlier)
        in_specs.append(IN_HBM)
    return pl.pallas_call(
        functools.partial(step_grad_kernel, by_rows, half, halves),
        grid=(1,),
        in_specs=in_specs,
        out_specs=out_spec,
        out_shape=jax.ShapeDtypeStruct(shape, F32),
        scratch_shapes=[
            pltpu.VMEM(scratch[0], BF16),
            pltpu.VMEM(scratch[1], OFFSET),
            pltpu.VMEM(scratch[2], BF16),
            pltpu.SemaphoreType.DMA((2,)),
            pltpu.SemaphoreType.DMA((COUNT,)),
        ],
        input_output_aliases=aliases,
        compiler_params=params(),
        cost_estimate=cost(8 * tokens * depth * width // halves, depth * width // halves),
    )(*operands)


class Side:
    def __init__(self, *jobs):
        self.jobs = list(jobs)

    def swap(self, value, bit):
        count = lax.axis_size("tensor")
        pairs = [(i, i ^ bit) for i in range(count)]
        job = self.jobs.pop(0) if self.jobs else None
        if job is None:
            return lax.ppermute(value, "tensor", pairs)
        call, operands, results = job
        value, operands = lax.optimization_barrier((value, operands))
        got = lax.ppermute(value, "tensor", pairs)
        found = call(*operands, results.get("value"))
        got, results["value"] = lax.optimization_barrier((got, found))
        return got


def own_bit(bit):
    return (lax.axis_index("tensor") // bit) % 2


def halve_first(side, kept, sent, bit):
    return kept, side.swap(sent, bit)


def halve(side, terms, bit):
    half = terms[0].shape[0] // 2
    mine = own_bit(bit)

    def part(place):
        one, other = (lax.dynamic_slice_in_dim(term, place * half, half, 0) for term in terms)
        return one.astype(F32) + other.astype(F32)

    return part(mine), side.swap(part(1 - mine).astype(BF16), bit)


def total(terms):
    return terms[0].astype(F32) + terms[1].astype(F32)


def add_up(side, value, bit):
    rounded = value.astype(BF16)
    return rounded.astype(F32) + side.swap(rounded, bit).astype(F32)


def double(side, value, bit, axis):
    other = side.swap(value, bit)
    mine = own_bit(bit) == 0
    return jnp.concatenate(
        [jnp.where(mine, value, other), jnp.where(mine, other, value)], axis=axis
    )


def inverse_rms(values):
    return lax.rsqrt(jnp.mean(values * values, axis=-1, keepdims=True) + norm_epsilon)


def norm_rows(state, gain):
    values = state.astype(F32)
    return (values * inverse_rms(values) * gain).astype(BF16)


def norm_back(state, gain, upstream):
    values = state.astype(F32)
    scale = inverse_rms(values)
    normal = values * scale
    inner = upstream * gain
    return scale * (inner - normal * jnp.mean(inner * normal, axis=-1, keepdims=True))


def token_lengths(doc_lengths, index_rows, micro_rows):
    batch_index = index_rows // micro_rows
    position = index_rows % micro_rows
    picked = batch_index[:, None] == jnp.arange(doc_lengths.shape[0], dtype=jnp.int32)[None, :]
    chosen = jnp.sum(jnp.where(picked[:, :, None], doc_lengths[None, :, :], 0), axis=1)
    ends = jnp.sum(
        jnp.where(
            jnp.arange(chosen.shape[1])[:, None] <= jnp.arange(chosen.shape[1])[None, :],
            chosen[:, :, None],
            0,
        ),
        axis=1,
    )
    starts = ends - chosen
    inside = (position[:, None] >= starts) & (position[:, None] < ends)
    return jnp.sum(jnp.where(inside, chosen, 0), axis=1).astype(F32)


def on_device(
    tokens,
    norm_gain,
    gate_codes,
    up_codes,
    down_codes,
    gate_zero,
    up_zero,
    down_zero,
    gate_step,
    up_step,
    down_step,
    out_grad,
    doc_lengths,
):
    shard_rows, features = tokens.shape
    device_count = lax.axis_size("tensor")
    micro_rows = shard_rows * device_count // doc_lengths.shape[0]
    bits = [1 << k for k in range(device_count.bit_length() - 1)]
    near, far = bits[:-2], bits[-2:]

    far_count = 1 << len(far)
    far_index = np.arange(far_count)
    far_place = sum(((far_index >> k) & 1) << (len(far) - 1 - k) for k in range(len(far)))
    far_device = np.argsort(far_place)
    near_part = lax.axis_index("tensor") % (1 << len(near))
    device_ids = near_part + jnp.asarray(far_device << len(near), jnp.int32)
    row_ids = (
        device_ids[:, None] * shard_rows + jnp.arange(shard_rows, dtype=jnp.int32)[None, :]
    ).reshape(-1)
    lengths = token_lengths(doc_lengths, row_ids, micro_rows)

    down_step, down_zero = down_step.transpose(1, 0, 2), down_zero.transpose(1, 0, 2)

    def offsets_jobs(codes, zeros, layer, unpack_half=offsets_of):
        results = {}
        call = lambda c, z, earlier: unpack_half(c, z, layer, earlier)
        return [(call, (codes, zeros), results)] * 2, results

    whole = functools.partial(offsets_of, halves=1)
    gate_jobs, gate_0 = offsets_jobs(gate_codes, gate_zero, 0)
    up_jobs, up_0 = offsets_jobs(up_codes, up_zero, 0, whole)
    side = Side(None, *gate_jobs, up_jobs[0])
    pair = jnp.stack([tokens, out_grad])
    for bit in reversed(far):
        pair = double(side, pair, bit, 1)
    state_0 = pair[0]
    cot_rows = (pair[1].astype(F32) / lengths[:, None]).astype(BF16)
    pair = jnp.stack([norm_rows(pair[0], norm_gain[0]), cot_rows])
    for bit in reversed(near):
        pair = double(side, pair, bit, 1)
    normed_0, cotangent = pair[0], pair[1]
    gate_0, up_0 = gate_0["value"], up_0["value"]

    mine = own_bit(near[0]).reshape(1).astype(jnp.int32)
    gate_pre, up_value, hidden_0, kept, sent, down_0 = first_forward(
        0, mine, normed_0, gate_0, up_0, down_codes, down_zero, gate_step, up_step, down_step
    )

    gate_jobs, gate_1 = offsets_jobs(gate_codes, gate_zero, 1)
    up_jobs, up_1 = offsets_jobs(up_codes, up_zero, 1)
    down_jobs, down_1 = offsets_jobs(down_codes, down_zero, 1, down_offsets_of)
    side = Side(None, gate_jobs[0], *down_jobs, gate_jobs[1], *up_jobs)
    part = halve_first(side, kept, sent, near[0])
    for bit in near[1:]:
        part = halve(side, part, bit)
    part = total(part)
    for bit in far:
        part = add_up(side, part, bit)
    state_1 = (state_0.astype(F32) + part).astype(BF16)
    normed_1 = norm_rows(state_1, norm_gain[1])
    for bit in reversed(near):
        normed_1 = double(side, normed_1, bit, 0)
    gate_1, up_1, down_1 = gate_1["value"], up_1["value"], down_1["value"]

    hidden_1, gate_grad, up_grad, kept, sent = last_layer(
        1, mine, normed_1, cotangent, gate_1, up_1, down_1, gate_step, up_step, down_step
    )

    down_out, gate_out, up_out = {}, {}, {}

    def half_jobs(x, offsets, upstream, results):
        return [
            (
                lambda x, u, earlier, half=half: step_grad(x, offsets, u, 1, half, 2, earlier),
                (x, upstream),
                results,
            )
            for half in range(2)
        ]

    side = Side(
        None,
        *half_jobs(hidden_1, down_1, cotangent, down_out),
        *half_jobs(normed_1, gate_1, gate_grad, gate_out),
        *half_jobs(normed_1, up_1, up_grad, up_out),
    )
    part = halve_first(side, kept, sent, near[0])
    for bit in near[1:]:
        part = halve(side, part, bit)
    part = total(part)
    for bit in far:
        part = add_up(side, part, bit)
    cot_rows = (cot_rows.astype(F32) + norm_back(state_1, norm_gain[1], part)).astype(BF16)
    cotangent = cot_rows
    for bit in reversed(near):
        cotangent = double(side, cotangent, bit, 0)

    gate_grad, up_grad, kept, sent = backward(
        0,
        mine,
        cotangent,
        gate_pre,
        up_value,
        gate_0,
        up_0,
        down_0,
        gate_step,
        up_step,
        down_step,
    )
    last = down_out["value"]
    down_out = {}
    side = Side(
        None,
        (
            lambda x, u, earlier: step_grad(x, down_0, u, 0, 0, 1, earlier, last),
            (hidden_0, cotangent),
            down_out,
        ),
        (
            lambda x, u, earlier: step_grad(x, gate_0, u, 0, 0, 1, earlier),
            (normed_0, gate_grad),
            gate_out,
        ),
        *[
            (
                lambda x, u, earlier, half=half: step_grad(x, up_0, u, 0, half, 2, earlier),
                (normed_0, up_grad),
                up_out,
            )
            for half in range(2)
        ],
    )
    part = halve_first(side, kept, sent, near[0])
    for bit in near[1:]:
        part = halve(side, part, bit)
    for bit in far:
        part = halve(side, part, bit)
        half = cot_rows.shape[0] // 2
        cot_rows = lax.dynamic_slice_in_dim(cot_rows, own_bit(bit) * half, half, 0)
    part = total(part)
    result = (cot_rows.astype(F32) + norm_back(tokens, norm_gain[0], part)).astype(BF16)
    return result, gate_out["value"], up_out["value"], down_out["value"].transpose(1, 0, 2)


def solution(mesh):
    placed = (
        P(("groups", "tensor"), None),
        P(),
        P(None, None, "tensor"),
        P(None, None, "tensor"),
        P(None, "tensor", None),
        P(None, None, "tensor"),
        P(None, None, "tensor"),
        P(None, "tensor", None),
        P(None, None, "tensor"),
        P(None, None, "tensor"),
        P(None, "tensor", None),
        P(("groups", "tensor"), None),
        P("groups", None),
    )
    return jax.shard_map(
        on_device,
        mesh=mesh,
        in_specs=placed,
        out_specs=(
            P(("groups", "tensor"), None),
            P("groups", None, "tensor"),
            P("groups", None, "tensor"),
            P("groups", "tensor", None),
        ),
        check_vma=False,
    )
```
